128 devices in a mesh: seq: 16 (over z, x), kvh: 8 (over y, core).
Axes of the slice: x: 4, y: 4, z: 4, core: 2. Of those that a mesh axis runs over, the one named last changes fastest.
Arguments:
- queries: bfloat16 [2048, 8, 1024], P('seq', 'kvh'), may hold values from -140 to 140
- kv_cache: bfloat16 [8, 131072, 256], P('kvh', 'seq'), may hold values from -6 to 6
- block_list: int32 [32, 64], replicated, may hold values from 0 to 2047, as said below
- out_weight: bfloat16 [8, 1024, 8192], P('kvh'), may hold values from -0.09375 to 0.09375
Outputs:
- projected: float32 [2048, 8192], P('seq', 'kvh')
The draws below stay inside these ranges and needn't reach their ends.
Inputs may be any that keep to these rules, and one draw needn't show every extreme that they name: `block_list`: each row names 64 different key blocks, none after its own query block's key block 2016 + row; it names that block and the 3 blocks before it; at most 16 of a row's blocks lie in one key group, and in every row exactly 16 lie in some key group other than the last.
All inputs are finite; a program needn't handle non-finite values.
Results may differ from the reference program's by a relative error of at most 0.0038.
Values may be sent and summed in bfloat16 or wider, within the bound.
No kernel may reach another device: no remote copies, remote signals or barrier semaphores. Data moves between devices by JAX's collectives and lax.ppermute only.
A program may use at most 128 MiB of HBM per device.

```python
import math
import jax
import jax.numpy as jnp
from jax import lax

D = 8192
HD = 128
GROUP = 8
KV_HEADS = 8
HEADS = 64
BLK = 64
Q_TOK = 2048
MOST = 16
SLASH = 4
SEL = 64
QB = 32
NB_DEV = 128
CACHE = 131072
NKB = 2048
N_SEQ = 16


def draw_block_list(key, part):
    key = jax.random.fold_in(key, 11)
    subkeys = jax.random.split(key, 5)
    others = N_SEQ - 2
    token_count = others * MOST
    remaining = SEL - MOST - SLASH
    hot_shard = jnp.minimum(jax.random.randint(subkeys[0], (QB,), 0, N_SEQ - 1), jax.random.randint(subkeys[1], (QB,), 0, N_SEQ - 1))
    token_score = jax.random.randint(subkeys[2], (QB, token_count), 0, 1 << 20) * token_count
    token_score = token_score + jnp.arange(token_count, dtype=jnp.int32)[None, :]
    picked = jnp.argsort(token_score, axis=1)[:, :remaining].astype(jnp.int32)
    token_shard = picked // MOST
    token_rank = picked % MOST
    shard_ids = token_shard + (token_shard >= hot_shard[:, None]).astype(jnp.int32)
    block_score = jax.random.randint(subkeys[3], (QB, N_SEQ - 1, NB_DEV), 0, 1 << 20) * NB_DEV
    block_score = block_score + jnp.arange(NB_DEV, dtype=jnp.int32)[None, None, :]
    orders = jnp.argsort(block_score, axis=2).astype(jnp.int32).reshape(QB, (N_SEQ - 1) * NB_DEV)
    other_local = jnp.take_along_axis(orders, shard_ids * NB_DEV + token_rank, axis=1)
    hot_local = jnp.take_along_axis(orders, hot_shard[:, None] * NB_DEV + jnp.arange(MOST, dtype=jnp.int32)[None, :], axis=1)
    other_ids = shard_ids * NB_DEV + other_local
    hot_ids = hot_shard[:, None] * NB_DEV + hot_local
    diagonal = (N_SEQ - 1) * NB_DEV + NB_DEV - QB + jnp.arange(QB, dtype=jnp.int32)
    slash_ids = diagonal[:, None] - jnp.arange(SLASH, dtype=jnp.int32)[None, :]
    joined = jnp.concatenate([hot_ids, other_ids, slash_ids], axis=1).astype(jnp.int32)
    shuffle = jax.random.randint(subkeys[4], (QB, SEL), 0, 1 << 20) * SEL + jnp.arange(SEL, dtype=jnp.int32)[None, :]
    mixing = jnp.argsort(shuffle, axis=1).astype(jnp.int32)
    return jnp.take_along_axis(joined, mixing, axis=1)


def draw_queries(key, part):
    key = jax.random.fold_in(key, 12)
    subkeys = jax.random.split(key, 1)
    values = jnp.clip(jax.random.normal(subkeys[0], (Q_TOK, KV_HEADS, GROUP, HD), jnp.float32), -6.0, 6.0)
    return values.reshape(Q_TOK, KV_HEADS, GROUP * HD).astype(jnp.bfloat16)


def spiked(drawn, key, source, target, shards_of, factor):
    def block_of(axis_at):
        return (jnp.arange(drawn.shape[axis_at]) // (drawn.shape[axis_at] // shards_of)).reshape((-1,) + (1,) * (drawn.ndim - 1 - axis_at))

    one_side = jax.random.permutation(key, shards_of)[block_of(target)]
    other_side = (block_of(target) + shards_of // 2) % shards_of
    return jnp.where((block_of(source) == one_side) | (block_of(source) == other_side), factor * drawn, drawn)


def level_of(own_key, dims, cuts, smallest, high):
    gain, own = 1.0, jax.random.fold_in(own_key, 6)
    for position, parts in cuts:
        steps = jnp.exp(jax.random.uniform(jax.random.fold_in(own, position), (parts,), jnp.float32, smallest / len(cuts), high / len(cuts)))
        gain = gain * jnp.repeat(steps, dims[position] // parts).reshape([-1 if axis == position else 1 for axis in range(len(dims))])
    return gain


def bell_draw(stream_key, shape, width, most, shards=(), kind=jnp.bfloat16):
    entries = width * jax.random.normal(stream_key, shape, jnp.float32)
    if shards:
        entries = entries * level_of(stream_key, shape, shards, -0.22, 0.18)
    return jnp.clip(entries, -most, most).astype(kind)


def gaussian_with(key, dims, spread, reach, shards, heavy, kind=jnp.bfloat16):
    result = spread * jax.random.normal(key, dims, jnp.float32)
    if shards:
        result = result * level_of(key, dims, shards, -0.22, 0.18)
    return jnp.clip(spiked(result, jax.random.fold_in(key, 3), *heavy), -reach, reach).astype(kind)


def setup_inputs(seed: int = 0) -> dict:
    key_of = jax.random.split(jax.random.key(seed), 5)
    return {
        "queries": draw_queries(jax.random.fold_in(key_of[4], 71), 0),
        "kv_cache": bell_draw(key_of[1], (KV_HEADS, CACHE, 2 * HD), 1.0, 6.0, ((0, 8), (1, 16))),
        "block_list": draw_block_list(jax.random.fold_in(key_of[4], 71), 0),
        "out_weight": gaussian_with(key_of[3], (KV_HEADS, GROUP * HD, D), (HEADS * HD) ** -0.5, 0.09375, ((0, 8),), (0, 2, 8, 2.0)),
    }


def reference(queries, kv_cache, block_list, out_weight):
    row_count = BLK * GROUP
    first_pos = CACHE - Q_TOK
    score_scale = 1.0 / math.sqrt(HD)
    shard_of = block_list // NB_DEV
    query_blocks = queries.reshape(QB, BLK, KV_HEADS, GROUP, HD)
    query_blocks = jnp.transpose(query_blocks, (2, 0, 1, 3, 4)).reshape(KV_HEADS * QB, row_count, HD)
    head_index = jnp.repeat(jnp.arange(KV_HEADS, dtype=jnp.int32), QB)
    block_index = jnp.tile(jnp.arange(QB, dtype=jnp.int32), KV_HEADS)

    def attend_block(inputs):
        head_now, block_now, query_rows = inputs
        block_ids = block_list[block_now]
        shard_ids = shard_of[block_now]
        cache_blocks = kv_cache[head_now].reshape(NKB, BLK, 2 * HD)
        fetched = cache_blocks[block_ids].astype(jnp.float32)
        key_part = fetched[:, :, :HD]
        value_part = fetched[:, :, HD:]
        scores = jnp.einsum('rd,skd->rsk', query_rows.astype(jnp.float32), key_part, precision=lax.Precision.HIGHEST) * score_scale
        query_pos = first_pos + block_now * BLK + jnp.arange(row_count, dtype=jnp.int32) // GROUP
        key_pos = block_ids[:, None] * BLK + jnp.arange(BLK, dtype=jnp.int32)[None, :]
        allowed = key_pos[None, :, :] <= query_pos[:, None, None]
        masked = jnp.where(allowed, scores, -1e+30)
        block_peak = lax.optimization_barrier(jnp.max(masked, axis=2))
        same_group = shard_ids[:, None] == shard_ids[None, :]
        group_peak = lax.optimization_barrier(jnp.max(jnp.where(same_group[None, :, :], block_peak[:, None, :], -1e+30), axis=2))
        row_top = lax.optimization_barrier(jnp.max(block_peak, axis=1))
        weights = jnp.where(allowed, jnp.exp(masked - group_peak[:, :, None]), 0.0)
        factors = jnp.exp(group_peak - row_top[:, None])
        rounded = lax.optimization_barrier(weights.astype(jnp.bfloat16)).astype(jnp.float32)
        numer = jnp.einsum('rsk,skd->rd', rounded * factors[:, :, None], value_part, precision=lax.Precision.HIGHEST)
        totals = lax.optimization_barrier(jnp.sum(weights * factors[:, :, None], axis=(1, 2)))
        return numer / totals[:, None]
    results = lax.map(attend_block, (head_index, block_index, query_blocks))
    results = results.reshape(KV_HEADS, QB, BLK, GROUP, HD)
    results = jnp.transpose(results, (1, 2, 0, 3, 4)).reshape(Q_TOK, HEADS * HD)
    attention = results.astype(jnp.bfloat16)
    flat_weight = out_weight.reshape(HEADS * HD, D)
    return jnp.dot(attention, flat_weight, preferred_element_type=jnp.float32)
```

```python
import functools
import math

import jax
import jax.numpy as jnp
from jax import lax
from jax.experimental import pallas as pl
from jax.experimental.pallas import tpu as pltpu
from jax.sharding import PartitionSpec as P

BLK = 64
MOST = 16
HD = 128
GROUP = 8
ROWS = BLK * GROUP
CHUNK = 4
PAY = HD + 16
NEG = -1e30
SCALE = 1.0 / math.sqrt(HD)
LOG2E = math.log2(math.e)
BF = jnp.bfloat16
F32 = jnp.float32


def seq_shift(dz, dx):
    return [(z * 4 + x, ((z + dz) % 4) * 4 + (x + dx) % 4) for z in range(4) for x in range(4)]


def kvh_shift(dy, dc):
    return [(y * 2 + c, ((y + dy) % 4) * 2 + (c + dc) % 2) for y in range(4) for c in range(2)]


def pack(numer, peak, total):
    high = total.astype(BF).astype(F32)
    low = total - high
    row = lax.broadcasted_iota(jnp.int32, (16, ROWS), 0)
    tail = jnp.where(row == 0, peak, jnp.where(row == 1, high, jnp.where(row == 2, low, 0.0)))
    return numer, tail


def attend_kernel(meta_ref, count_ref, ids_ref, kv_ref, *refs, parts, per):
    q_refs, out_refs = refs[:parts], refs[parts : 2 * parts]
    q_scr, o_scr, s_scr, acc = refs[2 * parts :]
    for i, q_ref in enumerate(q_refs):
        q_scr[i * per : (i + 1) * per] = q_ref[...]
    diag_here = meta_ref[parts * per]

    def one(t, carry):
        qb = meta_ref[t]
        n = count_ref[qb]
        chunks = (n + (CHUNK - 1)) // CHUNK
        q = jnp.concatenate([q_scr[t, :, g * HD : (g + 1) * HD] for g in range(GROUP)], axis=0)

        def fetch(c, lo):
            return jnp.concatenate(
                [
                    kv_ref[pl.ds(pl.multiple_of(ids_ref[qb * MOST + c * CHUNK + u] * BLK, BLK), BLK), lo : lo + HD]
                    for u in range(CHUNK)
                ],
                axis=0,
            )

        def first(c, peak):
            base = pl.multiple_of(c * CHUNK * BLK, CHUNK * BLK)
            s_scr[pl.ds(base, CHUNK * BLK), :] = lax.dot_general(
                fetch(c, 0), q, (((1,), (1,)), ((), ())), preferred_element_type=F32
            )

            @pl.when((c == 0) & (diag_here == 1))
            def _():
                off = lax.broadcasted_iota(jnp.int32, (BLK, ROWS), 0)
                tok = lax.broadcasted_iota(jnp.int32, (BLK, ROWS), 1) % BLK
                s_scr[0:BLK, :] = jnp.where(off <= tok, s_scr[0:BLK, :], NEG)

            for u in range(1, CHUNK):

                @pl.when(c * CHUNK + u >= n)
                def _(u=u):
                    s_scr[pl.ds(base + u * BLK, BLK), :] = jnp.full((BLK, ROWS), NEG, F32)

            s = s_scr[pl.ds(base, CHUNK * BLK), :]
            return jnp.maximum(peak, jnp.max(s.reshape(CHUNK * BLK // 8, 8, ROWS), axis=0))

        peak = lax.fori_loop(0, chunks, first, jnp.full((8, ROWS), NEG, F32))
        peak = jnp.max(peak, axis=0, keepdims=True)
        acc[...] = jnp.zeros_like(acc)

        def second(c, total):
            base = pl.multiple_of(c * CHUNK * BLK, CHUNK * BLK)
            s = s_scr[pl.ds(base, CHUNK * BLK), :]
            w = jnp.exp2((s - peak) * (SCALE * LOG2E))
            acc[...] += lax.dot_general(
                fetch(c, HD), w.astype(BF), (((0,), (0,)), ((), ())), preferred_element_type=F32
            )
            return total + jnp.sum(w.reshape(CHUNK * BLK // 8, 8, ROWS), axis=0)

        total = lax.fori_loop(0, chunks, second, jnp.zeros((8, ROWS), F32))
        total = jnp.sum(total, axis=0, keepdims=True)
        scaled = peak * SCALE
        near = scaled.astype(BF).astype(F32)
        gain = jnp.exp2(jnp.where(n > 0, scaled - near, 0.0) * LOG2E)
        numer, tail = pack(acc[...] * gain, near, total * gain)
        o_scr[t, :HD] = numer.astype(o_scr.dtype)
        o_scr[t, HD:] = tail.astype(o_scr.dtype)
        return carry

    lax.fori_loop(0, parts * per, one, 0)
    for i, out_ref in enumerate(out_refs):
        out_ref[...] = o_scr[i * per : (i + 1) * per]


VM = pl.BlockSpec(memory_space=pltpu.VMEM)
SM = pl.BlockSpec(memory_space=pltpu.SMEM)


def attend(qbs, diag_here, counts, ids, kv, arrays, dtype):
    parts, per = len(arrays), arrays[0].shape[0]
    meta = jnp.stack(qbs + [diag_here]).astype(jnp.int32)
    total = parts * per
    return pl.pallas_call(
        functools.partial(attend_kernel, parts=parts, per=per),
        out_shape=[jax.ShapeDtypeStruct((per, PAY, ROWS), dtype)] * parts,
        in_specs=[SM, SM, SM, VM] + [VM] * parts,
        out_specs=[VM] * parts,
        scratch_shapes=[
            pltpu.VMEM((total, BLK, GROUP * HD), BF),
            pltpu.VMEM((total, PAY, ROWS), dtype),
            pltpu.VMEM((MOST * BLK, ROWS), F32),
            pltpu.VMEM((HD, ROWS), F32),
        ],
        compiler_params=pltpu.CompilerParams(vmem_limit_bytes=40 * 2**20),
        cost_estimate=pl.CostEstimate(flops=total * 8 * 16777216, bytes_accessed=8 * 2**20, transcendentals=total * 8 * 32768),
        name="attend",
    )(meta, counts, ids, kv, *arrays)


def merge(blocks):
    tails = [b[HD:].astype(F32) for b in blocks]
    peaks = [t[0:1] for t in tails]
    top = functools.reduce(jnp.maximum, peaks)
    gains = [jnp.exp2((p - top) * LOG2E) for p in peaks]
    numer = sum(b[:HD].astype(F32) * g for b, g in zip(blocks, gains))
    total = sum((t[1:2] + t[2:3]) * g for t, g in zip(tails, gains))
    return numer, top, total


def stage_kernel(*refs):
    ins, outs = refs[:16], refs[16:]
    for half in range(2):
        for pair in range(2):
            srcs = ins[(half * 2 + pair) * 4 : (half * 2 + pair) * 4 + 4]
            for u in range(2):
                slot = pair * 2 + u
                numer, tail = pack(*merge([r[u] for r in srcs]))
                out = outs[half * 4 + slot]
                out[:HD] = numer.astype(out.dtype)
                out[HD:] = tail.astype(out.dtype)


def final_kernel(*refs):
    ins, out = refs[:8], refs[8]
    for half in range(2):
        numer, _, total = merge([r[...] for r in ins[half * 4 : half * 4 + 4]])
        att = numer / total
        for g in range(0, GROUP, 2):
            turned = att[:, g * BLK : (g + 2) * BLK].T.astype(BF)
            out[half * BLK : (half + 1) * BLK, g * HD : (g + 1) * HD] = turned[:BLK]
            out[half * BLK : (half + 1) * BLK, (g + 1) * HD : (g + 2) * HD] = turned[BLK:]


def local_call(kernel, out_shape, args, name):
    return pl.pallas_call(
        kernel,
        out_shape=out_shape,
        in_specs=[VM] * len(args),
        out_specs=jax.tree.map(lambda _: VM, out_shape),
        compiler_params=pltpu.CompilerParams(vmem_limit_bytes=40 * 2**20),
        cost_estimate=pl.CostEstimate(flops=10**7, bytes_accessed=6 * 2**20, transcendentals=0),
        name=name,
    )(*args)


COLS = 512


def project_kernel(idx_ref, att_ref, other_ref, w_ref, wo_ref, out_ref):
    out_ref[...] = (
        jnp.dot(att_ref[...], w_ref[...], preferred_element_type=F32)
        + jnp.dot(other_ref[...], wo_ref[...], preferred_element_type=F32)
    ).astype(out_ref.dtype)


def project(att, other, w, wo, mine, theirs, dtype):
    rows, depth = att.shape
    steps = 1024 // COLS
    idx = jnp.stack([mine, theirs]).astype(jnp.int32)
    return pl.pallas_call(
        project_kernel,
        out_shape=jax.ShapeDtypeStruct((rows, 1024), dtype),
        grid_spec=pltpu.PrefetchScalarGridSpec(
            num_scalar_prefetch=1,
            grid=(steps,),
            in_specs=[
                pl.BlockSpec((rows, depth), lambda i, idx: (0, 0)),
                pl.BlockSpec((rows, depth), lambda i, idx: (0, 0)),
                pl.BlockSpec((depth, COLS), lambda i, idx: (0, idx[0] * steps + i)),
                pl.BlockSpec((depth, COLS), lambda i, idx: (0, idx[1] * steps + i)),
            ],
            out_specs=pl.BlockSpec((rows, COLS), lambda i, idx: (0, i)),
        ),
        compiler_params=pltpu.CompilerParams(vmem_limit_bytes=40 * 2**20),
        cost_estimate=pl.CostEstimate(flops=2 * rows * 2 * depth * 1024, bytes_accessed=5 * 2**20, transcendentals=0),
        name="project",
    )(idx, att, other, w, wo)


def body(queries, kv_cache, block_list, out_weight):
    s = lax.axis_index("seq")
    z, x = s // 4, s % 4
    k = lax.axis_index("kvh")
    y, core = k // 2, k % 2
    kv = kv_cache[0]
    w = out_weight[0]
    block_count = kv.shape[0] // BLK
    qb_count = block_list.shape[0]

    def zx(v, dz, dx):
        return lax.ppermute(v, "seq", seq_shift(dz % 4, dx % 4))

    def yc(v, dy, dc):
        return lax.ppermute(v, "kvh", kvh_shift(dy % 4, dc))

    q = queries[:, 0, :].reshape(2, BLK, GROUP * HD)
    a0, b0 = q[0:1], q[1:2]
    a1, a3, a2 = zx(a0, 0, 1), zx(a0, 0, -1), zx(a0, 0, 2)
    b1, b3, b2 = zx(b0, 1, 0), zx(b0, -1, 0), zx(b0, 2, 0)

    w_split = w.reshape(w.shape[0], 4, 2, 1024)
    w_send = lax.dynamic_index_in_dim(w_split, 1 - core, axis=2, keepdims=False).reshape(w.shape[0], 4096)
    w_other = yc(w_send, 0, 1)

    last = lax.axis_size("seq") - 1
    own_ids = (last + 1) * block_count - qb_count + jnp.arange(qb_count, dtype=jnp.int32)
    diag_here = (s == last).astype(jnp.int32)
    mine = (block_list // block_count == s) & (block_list != own_ids[:, None])
    rank = jnp.cumsum(mine.astype(jnp.int32), axis=1) - 1 + diag_here
    counts = jnp.sum(mine.astype(jnp.int32), axis=1) + diag_here
    slots = jnp.arange(MOST, dtype=jnp.int32)
    hit = mine[:, :, None] & (rank[:, :, None] == slots[None, None, :])
    ids = jnp.sum(jnp.where(hit, (block_list % block_count)[:, :, None], 0), axis=1)
    ids = jnp.where((slots[None, :] == 0) & (diag_here == 1), (own_ids % block_count)[:, None], ids)
    ids = ids.reshape(-1)

    def qb_a(i, j):
        return 2 * (((z - i) % 4) * 4 + (x - j) % 4)

    def qb_b(i, j):
        return 2 * (((z - i) % 4) * 4 + (x - j) % 4) + 1

    a01, a23 = jnp.concatenate([a0, a1]), jnp.concatenate([a2, a3])
    b01, b23 = jnp.concatenate([b0, b1]), jnp.concatenate([b2, b3])
    au01, ad23 = zx(a01, 1, 0), zx(a23, -1, 0)
    bu01, bd23 = zx(b01, 0, 1), zx(b23, 0, -1)
    af01, af23 = zx(au01, 1, 0), zx(ad23, -1, 0)
    bf01, bf23 = zx(bu01, 0, 1), zx(bd23, 0, -1)
    au23, ad01 = zx(a23, 1, 0), zx(a01, -1, 0)
    bu23, bd01 = zx(b23, 0, 1), zx(b01, 0, -1)

    def run(arrays, steps, dtype):
        qbs = []
        for n, (far, pair) in enumerate(steps):
            for near in pair:
                qbs.append(qb_a(far, near) if n < 2 else qb_b(near, far))
        return attend(qbs, diag_here, counts, ids, kv, arrays, dtype)

    lo, hi = (0, 1), (2, 3)
    ao01, ao23, bo01, bo23 = run([a01, a23, b01, b23], [(0, lo), (0, hi)] * 2, F32)
    ra1_01, ra3_23, rb1_01, rb3_23 = run([au01, ad23, bu01, bd23], [(1, lo), (3, hi)] * 2, BF)
    ra2_01, ra2_23, rb2_01, rb2_23 = run([af01, af23, bf01, bf23], [(2, lo), (2, hi)] * 2, BF)
    ra1_23, ra3_01, rb1_23, rb3_01 = run([au23, ad01, bu23, bd01], [(1, hi), (3, lo)] * 2, BF)

    stage_in = [
        ao01, zx(ra1_01, -1, 0), zx(ra2_01, 2, 0), zx(ra3_01, 1, 0),
        ao23, zx(ra1_23, -1, 0), zx(zx(ra2_23, -1, 0), -1, 0), zx(ra3_23, 1, 0),
        bo01, zx(rb1_01, 0, -1), zx(rb2_01, 0, 2), zx(rb3_01, 0, 1),
        bo23, zx(rb1_23, 0, -1), zx(zx(rb2_23, 0, -1), 0, -1), zx(rb3_23, 0, 1),
    ]
    f_shape = jax.ShapeDtypeStruct((PAY, ROWS), F32)
    b_shape = jax.ShapeDtypeStruct((PAY, ROWS), BF)
    m = local_call(stage_kernel, [f_shape, b_shape, b_shape, b_shape] * 2, stage_in, "stage")
    final_in = [
        m[0], zx(m[1], 0, -1), zx(m[2], 0, 2), zx(m[3], 0, 1),
        m[4], zx(m[5], -1, 0), zx(m[6], 2, 0), zx(m[7], 1, 0),
    ]
    att = local_call(final_kernel, jax.ShapeDtypeStruct((2 * BLK, GROUP * HD), BF), final_in, "final")

    other = yc(att, 0, 1)

    def chunk(d, dtype):
        to = (y + d) % 4
        return project(att, other, w, w_other, 2 * to + core, to, dtype)

    r2 = yc(chunk(2, BF), 2, 0)
    r1 = yc(chunk(1, BF), 1, 0)
    r3 = yc(chunk(3, BF), 3, 0)
    return chunk(0, F32) + r1.astype(F32) + r2.astype(F32) + r3.astype(F32)


def solution(mesh):
    in_specs = (P("seq", "kvh", None), P("kvh", "seq", None), P(), P("kvh", None, None))
    out_specs = P("seq", "kvh")
    return jax.shard_map(body, mesh=mesh, in_specs=in_specs, out_specs=out_specs, check_vma=False)
```

```python
import functools
import math

import jax
import jax.numpy as jnp
from jax import lax
from jax.experimental import pallas as pl
from jax.experimental.pallas import tpu as pltpu
from jax.sharding import PartitionSpec as P

BLK = 64
MOST = 16
HD = 128
GROUP = 8
ROWS = BLK * GROUP
CHUNK = 4
FLIPS = (0, 1, 3, 2)
PAY = HD + 16
NEG = -1e30
SCALE = 1.0 / math.sqrt(HD)
LOG2E = math.log2(math.e)
BF = jnp.bfloat16
F32 = jnp.float32
COST = 8 * 10**9
VMEM_SOME = 20 * 2**20


def seq_shift(dz, dx):
    return [(z * 4 + x, ((z + dz) % 4) * 4 + (x + dx) % 4) for z in range(4) for x in range(4)]


def seq_flip(fz, fx):
    return [(z * 4 + x, (z ^ fz) * 4 + (x ^ fx)) for z in range(4) for x in range(4)]


def kvh_shift(dy, dc):
    return [(y * 2 + c, ((y + dy) % 4) * 2 + (c + dc) % 2) for y in range(4) for c in range(2)]


def pack(numer, peak, total):
    high = total.astype(BF).astype(F32)
    low = total - high
    row = lax.broadcasted_iota(jnp.int32, (16, ROWS), 0)
    tail = jnp.where(row == 0, peak, jnp.where(row == 1, high, jnp.where(row == 2, low, 0.0)))
    return numer, tail


def attend_kernel(place_ref, count_ref, ids_ref, kv_ref, *refs, far):
    parts, per = 2, 4
    q_refs, refs = refs[:parts], refs[parts:]
    out_refs, refs = refs[:parts], refs[parts:]
    q_scr, o_scr, s_scr, kv_scr, diag_scr, sems = refs
    total = parts * per
    pairs = total // 2
    step = CHUNK * BLK

    place = place_ref[0]
    z, x = place // 4, place % 4

    def qb_of(t):
        j = t % per
        f = j ^ (j // 2)
        qa = 2 * (((z + 4 - far) % 4) * 4 + (x ^ f))
        qb = 2 * ((z ^ f) * 4 + (x + 4 - far) % 4) + 1
        return jnp.where(t < per, qa, qb)

    def size(p):
        most = jnp.maximum(count_ref[qb_of(2 * p)], count_ref[qb_of(2 * p + 1)])
        return jnp.where(most <= CHUNK, 1, jnp.where(most <= 2 * CHUNK, 2, MOST // CHUNK))

    def start(p, slot):
        blocks = size(p) * CHUNK
        for u in range(2):
            base = qb_of(2 * p + u) * MOST

            def issue(v, carry, u=u, base=base):
                pltpu.make_async_copy(
                    kv_ref.at[pl.ds(pl.multiple_of(ids_ref[base + v] * BLK, BLK), BLK), :],
                    kv_scr.at[slot, u, pl.ds(pl.multiple_of(v * BLK, BLK), BLK), :],
                    sems.at[slot, u],
                ).start()
                return carry

            lax.fori_loop(0, blocks, issue, 0)

    start(0, 0)
    off = lax.broadcasted_iota(jnp.int32, (BLK, ROWS), 0)
    tok = lax.broadcasted_iota(jnp.int32, (BLK, ROWS), 1) % BLK
    diag_scr[...] = jnp.where((off > tok) & (place_ref[2] == 1), NEG, 0.0)
    for i, q_ref in enumerate(q_refs):
        q_scr[i * per : (i + 1) * per] = q_ref[...]

    def work(p, slot, chunks):
        counts = [count_ref[qb_of(2 * p + u)] for u in range(2)]
        for u in range(2):
            pltpu.make_async_copy(
                kv_ref.at[0 : chunks * step, :], kv_scr.at[slot, u, 0 : chunks * step, :], sems.at[slot, u]
            ).wait()
        peaks = []
        for u in range(2):
            q = jnp.concatenate([q_scr[2 * p + u, :, g * HD : (g + 1) * HD] for g in range(GROUP)], axis=0)
            peak = None
            for c in range(chunks):
                s = lax.dot_general(
                    kv_scr[slot, u, c * step : (c + 1) * step, :HD],
                    q,
                    (((1,), (1,)), ((), ())),
                    preferred_element_type=F32,
                )
                for v in range(CHUNK):
                    at = c * CHUNK + v
                    part = s[v * BLK : (v + 1) * BLK]
                    if at == 0:
                        part = part + diag_scr[...]
                    else:
                        part = part + jnp.where(at < counts[u], 0.0, NEG)
                    s_scr[u, at * BLK : (at + 1) * BLK, :] = part
                    part = jnp.max(part.reshape(BLK // 8, 8, ROWS), axis=0)
                    peak = part if peak is None else jnp.maximum(peak, part)
            peaks.append(jnp.max(peak, axis=0, keepdims=True))
        for u in range(2):
            peak = peaks[u]
            numer, mass = None, None
            for c in range(chunks):
                w = jnp.exp2((s_scr[u, c * step : (c + 1) * step, :] - peak) * (SCALE * LOG2E))
                part = lax.dot_general(
                    kv_scr[slot, u, c * step : (c + 1) * step, HD:],
                    w.astype(BF),
                    (((0,), (0,)), ((), ())),
                    preferred_element_type=F32,
                )
                numer = part if numer is None else numer + part
                part = jnp.sum(w.reshape(step // 8, 8, ROWS), axis=0)
                mass = part if mass is None else mass + part
            mass = jnp.sum(mass, axis=0, keepdims=True)
            used = counts[u] > 0
            scaled = peak * SCALE
            near = scaled.astype(BF).astype(F32)
            gain = jnp.where(used, jnp.exp2((scaled - near) * LOG2E), 0.0)
            near = jnp.where(used, near, NEG)
            numer, mass = numer * gain, mass * gain
            numer, tail = pack(numer, near, mass)
            o_scr[2 * p + u, :HD] = numer.astype(o_scr.dtype)
            o_scr[2 * p + u, HD:] = tail.astype(o_scr.dtype)

    def one(p, carry):
        slot = lax.rem(p, 2)

        @pl.when(p + 1 < pairs)
        def _():
            start(p + 1, 1 - slot)

        have = size(p)
        for chunks in (1, 2, MOST // CHUNK):

            @pl.when(have == chunks)
            def _(chunks=chunks):
                work(p, slot, chunks)

        return carry

    lax.fori_loop(0, pairs, one, 0)
    for i, out_ref in enumerate(out_refs):
        out_ref[...] = o_scr[i * per : (i + 1) * per]


VM = pl.BlockSpec(memory_space=pltpu.VMEM)
SM = pl.BlockSpec(memory_space=pltpu.SMEM)


HB = pl.BlockSpec(memory_space=pltpu.HBM)
WIDE = 1024


def attend(place, counts, ids, kv, arrays, far, dtype):
    parts, per = 2, 4
    total = parts * per
    return pl.pallas_call(
        functools.partial(attend_kernel, far=far),
        out_shape=[jax.ShapeDtypeStruct((per, PAY, ROWS), dtype)] * parts,
        in_specs=[SM, SM, SM, HB] + [VM] * parts,
        out_specs=[VM] * parts,
        scratch_shapes=[
            pltpu.VMEM((total, BLK, GROUP * HD), BF),
            pltpu.VMEM((total, PAY, ROWS), dtype),
            pltpu.VMEM((2, MOST * BLK, ROWS), F32),
            pltpu.VMEM((2, 2, MOST * BLK, 2 * HD), BF),
            pltpu.VMEM((BLK, ROWS), F32),
            pltpu.SemaphoreType.DMA((2, 2)),
        ],
        compiler_params=pltpu.CompilerParams(vmem_limit_bytes=VMEM_SOME),
        cost_estimate=pl.CostEstimate(flops=COST, bytes_accessed=2**20, transcendentals=0),
        name="attend",
    )(place, counts, ids, kv, *arrays)


def merge(blocks):
    tails = [b[HD:].astype(F32) for b in blocks]
    peaks = [t[0:1] for t in tails]
    top = functools.reduce(jnp.maximum, peaks)
    gains = [jnp.exp2((p - top) * LOG2E) for p in peaks]
    numer = sum(b[:HD].astype(F32) * g for b, g in zip(blocks, gains))
    total = sum((t[1:2] + t[2:3]) * g for t, g in zip(tails, gains))
    return numer, top, total


def store(out, at, numer, peak, total):
    numer, tail = pack(numer, peak, total)
    out[at, :HD] = numer.astype(out.dtype)
    out[at, HD:] = tail.astype(out.dtype)


def join_kernel(a_near, a_far, b_near, b_far, a_out, b_out):
    for near, far, out in ((a_near, a_far, a_out), (b_near, b_far, b_out)):
        for slot in range(4):
            store(out, slot, *merge([near[slot], far[slot]]))


def stage_kernel(*refs):
    ins, outs = refs[:6], refs[6:]
    for half in range(2):
        for slot in range(4):
            store(outs[half * 2 + slot // 2], slot % 2, *merge([r[slot] for r in ins[half * 3 : half * 3 + 3]]))


def step_kernel(*refs):
    ins, outs = refs[:4], refs[4:]
    for half in range(2):
        for slot in range(2):
            store(outs[half * 2 + slot], 0, *merge([r[slot] for r in ins[half * 2 : half * 2 + 2]]))


def final_kernel(*refs):
    ins, out = refs[:4], refs[4]
    for half in range(2):
        numer, _, total = merge([r[0] for r in ins[half * 2 : half * 2 + 2]])
        att = numer / total
        for g in range(0, GROUP, 2):
            turned = att[:, g * BLK : (g + 2) * BLK].T.astype(BF)
            out[half * BLK : (half + 1) * BLK, g * HD : (g + 1) * HD] = turned[:BLK]
            out[half * BLK : (half + 1) * BLK, (g + 1) * HD : (g + 2) * HD] = turned[BLK:]


def local_call(kernel, out_shape, args, name):
    return pl.pallas_call(
        kernel,
        out_shape=out_shape,
        in_specs=[VM] * len(args),
        out_specs=jax.tree.map(lambda _: VM, out_shape),
        compiler_params=pltpu.CompilerParams(vmem_limit_bytes=VMEM_SOME),
        cost_estimate=pl.CostEstimate(flops=10**7, bytes_accessed=2 * 2**20, transcendentals=0),
        name=name,
    )(*args)


def take_kernel(place_ref, w_ref, out_ref):
    out_ref[...] = w_ref[...]


def take_chunks(w, place):
    depth = w.shape[0]
    return pl.pallas_call(
        take_kernel,
        out_shape=jax.ShapeDtypeStruct((depth, 4 * WIDE), w.dtype),
        grid_spec=pltpu.PrefetchScalarGridSpec(
            num_scalar_prefetch=1,
            grid=(4,),
            in_specs=[pl.BlockSpec((depth, WIDE), lambda i, place: (0, i * 2 + 1 - place[1] % 2))],
            out_specs=pl.BlockSpec((depth, WIDE), lambda i, place: (0, i)),
        ),
        compiler_params=pltpu.CompilerParams(vmem_limit_bytes=52 * 2**20),
        cost_estimate=pl.CostEstimate(flops=0, bytes_accessed=16 * 2**20, transcendentals=0),
        name="take_chunks",
    )(place, w)


PIECE = 256


def project_kernel(place_ref, att_ref, other_ref, w_ref, wo_ref, out_ref, w_scr, acc, sems, *, far):
    k = place_ref[1]
    to = (k // 2 + far) % 4
    pieces = att_ref.shape[1] // PIECE
    copies = []
    for n, (ref, chunk) in enumerate([(w_ref, 2 * to + k % 2), (wo_ref, to)]):
        for r in range(pieces):
            copies.append(
                pltpu.make_async_copy(
                    ref.at[r * PIECE : (r + 1) * PIECE, pl.ds(pl.multiple_of(chunk * WIDE, WIDE), WIDE)],
                    w_scr.at[n * pieces + r],
                    sems.at[n * pieces + r],
                )
            )
    for c in copies:
        c.start()
    for n, ref in enumerate([att_ref, other_ref]):
        for r in range(pieces):
            at = n * pieces + r
            copies[at].wait()
            part = jnp.dot(ref[:, r * PIECE : (r + 1) * PIECE], w_scr[at], preferred_element_type=F32)
            if at == 0:
                acc[...] = part
            elif at < 2 * pieces - 1:
                acc[...] += part
            else:
                out_ref[...] = (acc[...] + part).astype(out_ref.dtype)


def project(place, att, other, w, wo, far, dtype):
    rows, depth = att.shape
    return pl.pallas_call(
        functools.partial(project_kernel, far=far),
        out_shape=jax.ShapeDtypeStruct((rows, WIDE), dtype),
        in_specs=[SM, VM, VM, HB, HB],
        out_specs=VM,
        scratch_shapes=[
            pltpu.VMEM((2 * depth // PIECE, PIECE, WIDE), BF),
            pltpu.VMEM((rows, WIDE), F32),
            pltpu.SemaphoreType.DMA((2 * depth // PIECE,)),
        ],
        compiler_params=pltpu.CompilerParams(vmem_limit_bytes=52 * 2**20),
        cost_estimate=pl.CostEstimate(flops=4 * rows * depth * WIDE, bytes_accessed=5 * 2**20, transcendentals=0),
        name="project",
    )(place, att, other, w, wo)


def body(queries, kv_cache, block_list, out_weight):
    s = lax.axis_index("seq")
    k = lax.axis_index("kvh")
    last = lax.axis_size("seq") - 1
    place = jnp.stack([s, k, jnp.where(s == last, 1, 0)]).astype(jnp.int32)
    kv = kv_cache[0]
    w = out_weight[0]
    block_count = kv.shape[0] // BLK
    qb_count = block_list.shape[0]

    def zx(v, dz, dx):
        return lax.ppermute(v, "seq", seq_shift(dz % 4, dx % 4))

    def flip(v, fz, fx):
        return lax.ppermute(v, "seq", seq_flip(fz, fx))

    def yc(v, dy, dc):
        return lax.ppermute(v, "kvh", kvh_shift(dy % 4, dc))

    q = queries[:, 0, :].reshape(2, BLK, GROUP * HD)
    a, b = q[0:1], q[1:2]
    a, b = lax.optimization_barrier((jnp.concatenate([a, flip(a, 0, 1)]), jnp.concatenate([b, flip(b, 1, 0)])))
    a, b = lax.optimization_barrier((jnp.concatenate([a, flip(a, 0, 3)]), jnp.concatenate([b, flip(b, 3, 0)])))
    w_send = take_chunks(lax.optimization_barrier((w, a, b))[0], place)
    w_other = yc(w_send, 0, 1)
    au, bu, ad, bd = lax.optimization_barrier((zx(a, 1, 0), zx(b, 0, 1), zx(a, -1, 0), zx(b, 0, -1)))
    af, bf = zx(au, 1, 0), zx(bu, 0, 1)

    own_ids = (last + 1) * block_count - qb_count + jnp.arange(qb_count, dtype=jnp.int32)
    diag_here = (s == last).astype(jnp.int32)
    mine = (block_list // block_count == s) & (block_list != own_ids[:, None])
    rank = jnp.cumsum(mine.astype(jnp.int32), axis=1) - 1 + diag_here
    counts = jnp.sum(mine.astype(jnp.int32), axis=1) + diag_here
    slots = jnp.arange(MOST, dtype=jnp.int32)
    hit = mine[:, :, None] & (rank[:, :, None] == slots[None, None, :])
    ids = jnp.sum(jnp.where(hit, (block_list % block_count)[:, :, None], 0), axis=1)
    ids = jnp.where((slots[None, :] == 0) & (diag_here == 1), (own_ids % block_count)[:, None], ids)
    ids = ids.reshape(-1)

    def run(pair, far, dtype):
        return attend(place, counts, ids, kv, pair, far, dtype)

    ra3, rb3 = run([ad, bd], 3, BF)
    ra3, rb3 = zx(ra3, 1, 0), zx(rb3, 0, 1)
    ra1, rb1 = run([au, bu], 1, F32)
    ra2, rb2 = run([af, bf], 2, BF)
    ra2, rb2 = zx(ra2, -1, 0), zx(rb2, 0, -1)
    ao, bo = run([a, b], 0, F32)
    b_four, b_two = (jax.ShapeDtypeStruct((n, PAY, ROWS), BF) for n in (4, 2))
    f_two = jax.ShapeDtypeStruct((2, PAY, ROWS), F32)
    b_one, f_one = (jax.ShapeDtypeStruct((1, PAY, ROWS), t) for t in (BF, F32))
    ra1, rb1 = local_call(join_kernel, [b_four] * 2, [ra1, ra2, rb1, rb2], "join")
    ra1, rb1 = zx(ra1, -1, 0), zx(rb1, 0, -1)
    a_stay, a_go, b_stay, b_go = local_call(
        stage_kernel, [f_two, b_two] * 2, [ao, ra3, ra1, bo, rb3, rb1], "stage"
    )
    a_go, b_go = flip(a_go, 0, 3), flip(b_go, 3, 0)
    a_stay, a_go, b_stay, b_go = local_call(step_kernel, [f_one, b_one] * 2, [a_stay, a_go, b_stay, b_go], "step")
    a_go, b_go = flip(a_go, 0, 1), flip(b_go, 1, 0)
    att = local_call(
        final_kernel, jax.ShapeDtypeStruct((2 * BLK, GROUP * HD), BF), [a_stay, a_go, b_stay, b_go], "final"
    )

    other = yc(att, 0, 1)

    def chunk(far, dtype):
        return project(place, att, other, w, w_other, far, dtype)

    r2 = yc(chunk(2, BF), 2, 0)
    r1 = yc(chunk(1, BF), 1, 0)
    r3 = yc(chunk(3, BF), 3, 0)
    return chunk(0, F32) + r1.astype(F32) + r2.astype(F32) + r3.astype(F32)


def solution(mesh):
    in_specs = (P("seq", "kvh", None), P("kvh", "seq", None), P(), P("kvh", None, None))
    out_specs = P("seq", "kvh")
    return jax.shard_map(body, mesh=mesh, in_specs=in_specs, out_specs=out_specs, check_vma=False)
```

```python
import functools
import math

import jax
import jax.numpy as jnp
from jax import lax
from jax.experimental import pallas as pl
from jax.experimental.pallas import tpu as pltpu
from jax.sharding import PartitionSpec as P

BLK = 64
MOST = 16
HD = 128
GROUP = 8
ROWS = BLK * GROUP
CHUNK = 4
FLIPS = (0, 1, 3, 2)
PAY = HD + 16
NEG = -1e30
SCALE = 1.0 / math.sqrt(HD)
LOG2E = math.log2(math.e)
BF = jnp.bfloat16
F32 = jnp.float32
COST = 4 * 10**9
VMEM_SOME = 16 * 2**20


def seq_shift(dz, dx):
    return [(z * 4 + x, ((z + dz) % 4) * 4 + (x + dx) % 4) for z in range(4) for x in range(4)]


def seq_flip(fz, fx):
    return [(z * 4 + x, (z ^ fz) * 4 + (x ^ fx)) for z in range(4) for x in range(4)]


def kvh_shift(dy, dc):
    return [(y * 2 + c, ((y + dy) % 4) * 2 + (c + dc) % 2) for y in range(4) for c in range(2)]


def pack(numer, peak, total):
    high = total.astype(BF).astype(F32)
    low = total - high
    row = lax.broadcasted_iota(jnp.int32, (16, ROWS), 0)
    tail = jnp.where(row == 0, peak, jnp.where(row == 1, high, jnp.where(row == 2, low, 0.0)))
    return numer, tail


def attend_kernel(place_ref, count_ref, ids_ref, kv_ref, *refs, far, cut):
    parts, per = 2, 4
    q_refs, refs = refs[:parts], refs[parts:]
    out_refs, refs = refs[: parts * cut], refs[parts * cut :]
    q_scr, o_scr, s_scr, diag_scr = refs
    total = parts * per
    pairs = total // 2
    step = CHUNK * BLK

    place = place_ref[0]
    z, x = place // 4, place % 4

    def qb_of(t):
        j = t % per
        f = j ^ (j // 2)
        qa = 2 * (((z + 4 - far) % 4) * 4 + (x ^ f))
        qb = 2 * ((z ^ f) * 4 + (x + 4 - far) % 4) + 1
        return jnp.where(t < per, qa, qb)

    def size(p):
        most = jnp.maximum(count_ref[qb_of(2 * p)], count_ref[qb_of(2 * p + 1)])
        return jnp.where(most <= CHUNK, 1, jnp.where(most <= 2 * CHUNK, 2, MOST // CHUNK))

    off = lax.broadcasted_iota(jnp.int32, (BLK, ROWS), 0)
    tok = lax.broadcasted_iota(jnp.int32, (BLK, ROWS), 1) % BLK
    diag_scr[...] = jnp.where((off > tok) & (place_ref[2] == 1), NEG, 0.0)
    for i, q_ref in enumerate(q_refs):
        q_scr[i * per : (i + 1) * per] = q_ref[...]

    def work(p, chunks):
        qbs = [qb_of(2 * p + u) for u in range(2)]
        counts = [count_ref[qb] for qb in qbs]

        def fetch(u, c, lo):
            ids = [ids_ref[qbs[u] * MOST + c * CHUNK + v] for v in range(CHUNK)]
            return jnp.concatenate(
                [kv_ref[pl.ds(pl.multiple_of(i * BLK, BLK), BLK), lo : lo + HD] for i in ids], axis=0
            )

        peaks = []
        for u in range(2):
            q = jnp.concatenate([q_scr[2 * p + u, :, g * HD : (g + 1) * HD] for g in range(GROUP)], axis=0)
            peak = None
            for c in range(chunks):
                s = lax.dot_general(
                    fetch(u, c, 0),
                    q,
                    (((1,), (1,)), ((), ())),
                    preferred_element_type=F32,
                )
                for v in range(CHUNK):
                    at = c * CHUNK + v
                    part = s[v * BLK : (v + 1) * BLK]
                    if at == 0:
                        part = part + diag_scr[...]
                    else:
                        part = part + jnp.where(at < counts[u], 0.0, NEG)
                    s_scr[u, at * BLK : (at + 1) * BLK, :] = part
                    part = jnp.max(part.reshape(BLK // 8, 8, ROWS), axis=0)
                    peak = part if peak is None else jnp.maximum(peak, part)
            peaks.append(jnp.max(peak, axis=0, keepdims=True))
        for u in range(2):
            peak = peaks[u]
            numer, mass = None, None
            for c in range(chunks):
                w = jnp.exp2((s_scr[u, c * step : (c + 1) * step, :] - peak) * (SCALE * LOG2E))
                part = lax.dot_general(
                    fetch(u, c, HD),
                    w.astype(BF),
                    (((0,), (0,)), ((), ())),
                    preferred_element_type=F32,
                )
                numer = part if numer is None else numer + part
                part = jnp.sum(w.reshape(step // 8, 8, ROWS), axis=0)
                mass = part if mass is None else mass + part
            mass = jnp.sum(mass, axis=0, keepdims=True)
            used = counts[u] > 0
            scaled = peak * SCALE
            near = scaled.astype(BF).astype(F32)
            gain = jnp.where(used, jnp.exp2((scaled - near) * LOG2E), 0.0)
            near = jnp.where(used, near, NEG)
            numer, mass = numer * gain, mass * gain
            numer, tail = pack(numer, near, mass)
            o_scr[2 * p + u, :HD] = numer.astype(o_scr.dtype)
            o_scr[2 * p + u, HD:] = tail.astype(o_scr.dtype)

    def one(p, carry):
        have = size(p)
        for chunks in (1, 2, MOST // CHUNK):

            @pl.when(have == chunks)
            def _(chunks=chunks):
                work(p, chunks)

        return carry

    lax.fori_loop(0, pairs, one, 0)
    for i, out_ref in enumerate(out_refs):
        out_ref[...] = o_scr[i * per // cut : (i + 1) * per // cut]


VM = pl.BlockSpec(memory_space=pltpu.VMEM)
SM = pl.BlockSpec(memory_space=pltpu.SMEM)


HB = pl.BlockSpec(memory_space=pltpu.HBM)
WIDE = 1024


def attend(place, counts, ids, kv, arrays, far, dtype, cut):
    parts, per = 2, 4
    total = parts * per
    return pl.pallas_call(
        functools.partial(attend_kernel, far=far, cut=cut),
        out_shape=[jax.ShapeDtypeStruct((per // cut, PAY, ROWS), dtype)] * (parts * cut),
        in_specs=[SM, SM, SM, VM] + [VM] * parts,
        out_specs=[VM] * (parts * cut),
        scratch_shapes=[
            pltpu.VMEM((total, BLK, GROUP * HD), BF),
            pltpu.VMEM((total, PAY, ROWS), dtype),
            pltpu.VMEM((2, MOST * BLK, ROWS), F32),
            pltpu.VMEM((BLK, ROWS), F32),
        ],
        compiler_params=pltpu.CompilerParams(vmem_limit_bytes=VMEM_SOME),
        cost_estimate=pl.CostEstimate(flops=COST, bytes_accessed=2**20, transcendentals=0),
        name="attend",
    )(place, counts, ids, kv, *arrays)


def merge(blocks):
    tails = [b[HD:].astype(F32) for b in blocks]
    peaks = [t[0:1] for t in tails]
    top = functools.reduce(jnp.maximum, peaks)
    gains = [jnp.exp2((p - top) * LOG2E) for p in peaks]
    numer = sum(b[:HD].astype(F32) * g for b, g in zip(blocks, gains))
    total = sum((t[1:2] + t[2:3]) * g for t, g in zip(tails, gains))
    return numer, top, total


def store(out, at, numer, peak, total):
    numer, tail = pack(numer, peak, total)
    out[at, :HD] = numer.astype(out.dtype)
    out[at, HD:] = tail.astype(out.dtype)


def join_kernel(*refs):
    ins, outs = refs[:8], refs[8:]
    for half in range(2):
        low, high, far_lo, far_hi = ins[half * 4 : half * 4 + 4]
        low_out, high_out = outs[half * 2 : half * 2 + 2]
        for slot in range(4):
            store(low_out, slot, *merge([low[slot], far_lo[slot]] if slot < 2 else [low[slot]]))
            store(high_out, slot, *merge([high[slot], far_hi[slot - 2]] if slot > 1 else [high[slot]]))


def stage_kernel(*refs):
    ins, outs = refs[:6], refs[6:]
    for half in range(2):
        for slot in range(4):
            store(outs[half * 4 + slot], 0, *merge([r[slot] for r in ins[half * 3 : half * 3 + 3]]))


def final_kernel(*refs):
    ins, out = refs[:8], refs[8]
    for half in range(2):
        numer, _, total = merge([r[0] for r in ins[half * 4 : half * 4 + 4]])
        att = numer / total
        for g in range(0, GROUP, 2):
            turned = att[:, g * BLK : (g + 2) * BLK].T.astype(BF)
            out[half * BLK : (half + 1) * BLK, g * HD : (g + 1) * HD] = turned[:BLK]
            out[half * BLK : (half + 1) * BLK, (g + 1) * HD : (g + 2) * HD] = turned[BLK:]


def local_call(kernel, out_shape, args, name):
    return pl.pallas_call(
        kernel,
        out_shape=out_shape,
        in_specs=[VM] * len(args),
        out_specs=jax.tree.map(lambda _: VM, out_shape),
        compiler_params=pltpu.CompilerParams(vmem_limit_bytes=VMEM_SOME),
        cost_estimate=pl.CostEstimate(flops=10**7, bytes_accessed=2 * 2**20, transcendentals=0),
        name=name,
    )(*args)


def project_kernel(place_ref, att_ref, other_ref, w_ref, wo_ref, *refs, fars):
    out_refs, (wo_scr, sems) = refs[: len(fars)], refs[len(fars) :]
    k = place_ref[1]
    cols = [pl.ds(pl.multiple_of((2 * ((k // 2 + far) % 4) + k % 2) * WIDE, WIDE), WIDE) for far in fars]
    copies = [pltpu.make_async_copy(wo_ref.at[:, c], wo_scr.at[n], sems.at[n]) for n, c in enumerate(cols)]
    for copy in copies:
        copy.start()
    for c, copy, wo, out_ref in zip(cols, copies, range(len(fars)), out_refs):
        value = jnp.dot(att_ref[...], w_ref[:, c], preferred_element_type=F32)
        copy.wait()
        value = value + jnp.dot(other_ref[...], wo_scr[wo], preferred_element_type=F32)
        out_ref[...] = value.astype(out_ref.dtype)


def project(place, att, other, w, wo, fars, dtypes):
    rows, depth = att.shape
    return pl.pallas_call(
        functools.partial(project_kernel, fars=fars),
        out_shape=[jax.ShapeDtypeStruct((rows, WIDE), t) for t in dtypes],
        in_specs=[SM, VM, VM, VM, HB],
        out_specs=[VM] * len(fars),
        scratch_shapes=[
            pltpu.VMEM((len(fars), depth, WIDE), BF),
            pltpu.SemaphoreType.DMA((len(fars),)),
        ],
        compiler_params=pltpu.CompilerParams(vmem_limit_bytes=30 * 2**20),
        cost_estimate=pl.CostEstimate(flops=2 * 10**9 * len(fars), bytes_accessed=2**20, transcendentals=0),
        name="project",
    )(place, att, other, w, wo)


def body(queries, kv_cache, block_list, out_weight):
    s = lax.axis_index("seq")
    k = lax.axis_index("kvh")
    last = lax.axis_size("seq") - 1
    place = jnp.stack([s, k, jnp.where(s == last, 1, 0)]).astype(jnp.int32)
    kv = kv_cache[0]
    w = out_weight[0]
    block_count = kv.shape[0] // BLK
    qb_count = block_list.shape[0]

    def zx(v, dz, dx):
        return lax.ppermute(v, "seq", seq_shift(dz % 4, dx % 4))

    def flip(v, fz, fx):
        return lax.ppermute(v, "seq", seq_flip(fz, fx))

    def yc(v, dy, dc):
        return lax.ppermute(v, "kvh", kvh_shift(dy % 4, dc))

    w_other = yc(w, 0, 1)

    q = queries[:, 0, :].reshape(2, BLK, GROUP * HD)
    a, b = q[0:1], q[1:2]
    a, b = lax.optimization_barrier((jnp.concatenate([a, flip(a, 0, 1)]), jnp.concatenate([b, flip(b, 1, 0)])))
    a, b = lax.optimization_barrier((jnp.concatenate([a, flip(a, 0, 3)]), jnp.concatenate([b, flip(b, 3, 0)])))
    au, bu, ad, bd = lax.optimization_barrier((zx(a, 1, 0), zx(b, 0, 1), zx(a, -1, 0), zx(b, 0, -1)))
    af, bf = zx(au, 1, 0), zx(bu, 0, 1)

    own_ids = (last + 1) * block_count - qb_count + jnp.arange(qb_count, dtype=jnp.int32)
    diag_here = (s == last).astype(jnp.int32)
    mine = (block_list // block_count == s) & (block_list != own_ids[:, None])
    rank = jnp.cumsum(mine.astype(jnp.int32), axis=1) - 1 + diag_here
    counts = jnp.sum(mine.astype(jnp.int32), axis=1) + diag_here
    slots = jnp.arange(MOST, dtype=jnp.int32)
    hit = mine[:, :, None] & (rank[:, :, None] == slots[None, None, :])
    ids = jnp.sum(jnp.where(hit, (block_list % block_count)[:, :, None], 0), axis=1)
    ids = jnp.where((slots[None, :] == 0) & (diag_here == 1), (own_ids % block_count)[:, None], ids)
    ids = ids.reshape(-1)

    def run(pair, far, dtype, cut=1):
        return attend(place, counts, ids, kv, pair, far, dtype, cut)

    ra1, rb1 = run([au, bu], 1, F32)
    ra3, rb3 = run([ad, bd], 3, F32)
    ra2_lo, ra2_hi, rb2_lo, rb2_hi = run([af, bf], 2, BF, 2)
    ra2_lo, ra2_hi = zx(ra2_lo, -1, 0), zx(ra2_hi, 1, 0)
    rb2_lo, rb2_hi = zx(rb2_lo, 0, -1), zx(rb2_hi, 0, 1)
    ao, bo = run([a, b], 0, F32)
    b_four, b_one = (jax.ShapeDtypeStruct((n, PAY, ROWS), BF) for n in (4, 1))
    f_one = jax.ShapeDtypeStruct((1, PAY, ROWS), F32)
    ra1, ra3, rb1, rb3 = local_call(
        join_kernel, [b_four] * 4, [ra1, ra3, ra2_lo, ra2_hi, rb1, rb3, rb2_lo, rb2_hi], "join"
    )
    ra1, rb1, ra3, rb3 = zx(ra1, -1, 0), zx(rb1, 0, -1), zx(ra3, 1, 0), zx(rb3, 0, 1)
    stage_in = [ao, ra3, ra1, bo, rb3, rb1]
    m = local_call(stage_kernel, [f_one, b_one, b_one, b_one] * 2, stage_in, "stage")
    final_in = [m[0]] + [flip(m[n], 0, FLIPS[n]) for n in (1, 2, 3)]
    final_in += [m[4]] + [flip(m[4 + n], FLIPS[n], 0) for n in (1, 2, 3)]
    att = local_call(final_kernel, jax.ShapeDtypeStruct((2 * BLK, GROUP * HD), BF), final_in, "final")

    other = yc(att, 0, 1)

    (p2,) = project(place, att, other, w, w_other, (2,), (BF,))
    r2 = yc(p2, 2, 0)
    p1, p3, own = project(place, att, other, w, w_other, (1, 3, 0), (BF, BF, F32))
    r1, r3 = yc(p1, 1, 0), yc(p3, 3, 0)
    return own + r1.astype(F32) + r2.astype(F32) + r3.astype(F32)


def solution(mesh):
    in_specs = (P("seq", "kvh", None), P("kvh", "seq", None), P(), P("kvh", None, None))
    out_specs = P("seq", "kvh")
    return jax.shard_map(body, mesh=mesh, in_specs=in_specs, out_specs=out_specs, check_vma=False)
```

```python
import functools
import math

import jax
import jax.numpy as jnp
from jax import lax
from jax.experimental import pallas as pl
from jax.experimental.pallas import tpu as pltpu
from jax.sharding import PartitionSpec as P

BLK = 64
MOST = 16
HD = 128
GROUP = 8
ROWS = BLK * GROUP
CHUNK = 4
FLIPS = (0, 1, 3, 2)
PAY = HD + 16
NEG = -1e30
SCALE = 1.0 / math.sqrt(HD)
LOG2E = math.log2(math.e)
BF = jnp.bfloat16
F32 = jnp.float32
COST = 4 * 10**9
VMEM_SOME = 16 * 2**20


def seq_shift(dz, dx):
    return [(z * 4 + x, ((z + dz) % 4) * 4 + (x + dx) % 4) for z in range(4) for x in range(4)]


def seq_flip(fz, fx):
    return [(z * 4 + x, (z ^ fz) * 4 + (x ^ fx)) for z in range(4) for x in range(4)]


def kvh_shift(dy, dc):
    return [(y * 2 + c, ((y + dy) % 4) * 2 + (c + dc) % 2) for y in range(4) for c in range(2)]


def pack(numer, peak, total):
    high = total.astype(BF).astype(F32)
    low = total - high
    row = lax.broadcasted_iota(jnp.int32, (16, ROWS), 0)
    tail = jnp.where(row == 0, peak, jnp.where(row == 1, high, jnp.where(row == 2, low, 0.0)))
    return numer, tail


def attend_kernel(place_ref, count_ref, ids_ref, kv_ref, *refs, far, cut):
    parts, per = 2, 4
    q_refs, refs = refs[:parts], refs[parts:]
    out_refs, refs = refs[: parts * cut], refs[parts * cut :]
    q_scr, o_scr, s_scr, diag_scr = refs
    total = parts * per
    pairs = total // 2
    step = CHUNK * BLK

    place = place_ref[0]
    z, x = place // 4, place % 4

    def qb_of(t):
        j = t % per
        f = j ^ (j // 2)
        qa = 2 * (((z + 4 - far) % 4) * 4 + (x ^ f))
        qb = 2 * ((z ^ f) * 4 + (x + 4 - far) % 4) + 1
        return jnp.where(t < per, qa, qb)

    def size(p):
        most = jnp.maximum(count_ref[qb_of(2 * p)], count_ref[qb_of(2 * p + 1)])
        return jnp.where(most <= CHUNK, 1, jnp.where(most <= 2 * CHUNK, 2, MOST // CHUNK))

    off = lax.broadcasted_iota(jnp.int32, (BLK, ROWS), 0)
    tok = lax.broadcasted_iota(jnp.int32, (BLK, ROWS), 1) % BLK
    diag_scr[...] = jnp.where((off > tok) & (place_ref[2] == 1), NEG, 0.0)
    for i, q_ref in enumerate(q_refs):
        q_scr[i * per : (i + 1) * per] = q_ref[...]

    def work(p, chunks):
        qbs = [qb_of(2 * p + u) for u in range(2)]
        counts = [count_ref[qb] for qb in qbs]

        def fetch(u, c, lo):
            ids = [ids_ref[qbs[u] * MOST + c * CHUNK + v] for v in range(CHUNK)]
            return jnp.concatenate(
                [kv_ref[pl.ds(pl.multiple_of(i * BLK, BLK), BLK), lo : lo + HD] for i in ids], axis=0
            )

        peaks = []
        for u in range(2):
            q = jnp.concatenate([q_scr[2 * p + u, :, g * HD : (g + 1) * HD] for g in range(GROUP)], axis=0)
            peak = None
            for c in range(chunks):
                s = lax.dot_general(
                    fetch(u, c, 0),
                    q,
                    (((1,), (1,)), ((), ())),
                    preferred_element_type=F32,
                )
                for v in range(CHUNK):
                    at = c * CHUNK + v
                    part = s[v * BLK : (v + 1) * BLK]
                    if at == 0:
                        part = part + diag_scr[...]
                    else:
                        part = part + jnp.where(at < counts[u], 0.0, NEG)
                    s_scr[u, at * BLK : (at + 1) * BLK, :] = part
                    part = jnp.max(part.reshape(BLK // 8, 8, ROWS), axis=0)
                    peak = part if peak is None else jnp.maximum(peak, part)
            peaks.append(jnp.max(peak, axis=0, keepdims=True))
        for u in range(2):
            peak = peaks[u]
            numer, mass = None, None
            for c in range(chunks):
                w = jnp.exp2((s_scr[u, c * step : (c + 1) * step, :] - peak) * (SCALE * LOG2E))
                part = lax.dot_general(
                    fetch(u, c, HD),
                    w.astype(BF),
                    (((0,), (0,)), ((), ())),
                    preferred_element_type=F32,
                )
                numer = part if numer is None else numer + part
                part = jnp.sum(w.reshape(step // 8, 8, ROWS), axis=0)
                mass = part if mass is None else mass + part
            mass = jnp.sum(mass, axis=0, keepdims=True)
            used = counts[u] > 0
            scaled = peak * SCALE
            near = scaled.astype(BF).astype(F32)
            gain = jnp.where(used, jnp.exp2((scaled - near) * LOG2E), 0.0)
            near = jnp.where(used, near, NEG)
            numer, mass = numer * gain, mass * gain
            numer, tail = pack(numer, near, mass)
            o_scr[2 * p + u, :HD] = numer.astype(o_scr.dtype)
            o_scr[2 * p + u, HD:] = tail.astype(o_scr.dtype)

    def one(p, carry):
        have = size(p)
        for chunks in (1, 2, MOST // CHUNK):

            @pl.when(have == chunks)
            def _(chunks=chunks):
                work(p, chunks)

        return carry

    lax.fori_loop(0, pairs, one, 0)
    for i, out_ref in enumerate(out_refs):
        out_ref[...] = o_scr[i * per // cut : (i + 1) * per // cut]


VM = pl.BlockSpec(memory_space=pltpu.VMEM)
SM = pl.BlockSpec(memory_space=pltpu.SMEM)


HB = pl.BlockSpec(memory_space=pltpu.HBM)
WIDE = 1024


def attend(place, counts, ids, kv, arrays, far, dtype, cut):
    parts, per = 2, 4
    total = parts * per
    return pl.pallas_call(
        functools.partial(attend_kernel, far=far, cut=cut),
        out_shape=[jax.ShapeDtypeStruct((per // cut, PAY, ROWS), dtype)] * (parts * cut),
        in_specs=[SM, SM, SM, VM] + [VM] * parts,
        out_specs=[VM] * (parts * cut),
        scratch_shapes=[
            pltpu.VMEM((total, BLK, GROUP * HD), BF),
            pltpu.VMEM((total, PAY, ROWS), dtype),
            pltpu.VMEM((2, MOST * BLK, ROWS), F32),
            pltpu.VMEM((BLK, ROWS), F32),
        ],
        compiler_params=pltpu.CompilerParams(vmem_limit_bytes=VMEM_SOME),
        cost_estimate=pl.CostEstimate(flops=COST, bytes_accessed=2**20, transcendentals=0),
        name="attend",
    )(place, counts, ids, kv, *arrays)


def merge(blocks):
    tails = [b[HD:].astype(F32) for b in blocks]
    peaks = [t[0:1] for t in tails]
    top = functools.reduce(jnp.maximum, peaks)
    gains = [jnp.exp2((p - top) * LOG2E) for p in peaks]
    numer = sum(b[:HD].astype(F32) * g for b, g in zip(blocks, gains))
    total = sum((t[1:2] + t[2:3]) * g for t, g in zip(tails, gains))
    return numer, top, total


def store(out, at, numer, peak, total):
    numer, tail = pack(numer, peak, total)
    out[at, :HD] = numer.astype(out.dtype)
    out[at, HD:] = tail.astype(out.dtype)


def join_kernel(*refs):
    ins, outs = refs[:8], refs[8:]
    for half in range(2):
        low, high, far_lo, far_hi = ins[half * 4 : half * 4 + 4]
        low_out, high_out = outs[half * 2 : half * 2 + 2]
        for slot in range(4):
            store(low_out, slot, *merge([low[slot], far_lo[slot]] if slot < 2 else [low[slot]]))
            store(high_out, slot, *merge([high[slot], far_hi[slot - 2]] if slot > 1 else [high[slot]]))


def stage_kernel(*refs):
    ins, outs = refs[:6], refs[6:]
    for half in range(2):
        for slot in range(4):
            store(outs[half * 4 + slot], 0, *merge([r[slot] for r in ins[half * 3 : half * 3 + 3]]))


def final_kernel(*refs):
    ins, out = refs[:8], refs[8]
    for half in range(2):
        numer, _, total = merge([r[0] for r in ins[half * 4 : half * 4 + 4]])
        att = numer / total
        for g in range(0, GROUP, 2):
            turned = att[:, g * BLK : (g + 2) * BLK].T.astype(BF)
            out[half * BLK : (half + 1) * BLK, g * HD : (g + 1) * HD] = turned[:BLK]
            out[half * BLK : (half + 1) * BLK, (g + 1) * HD : (g + 2) * HD] = turned[BLK:]


def local_call(kernel, out_shape, args, name):
    return pl.pallas_call(
        kernel,
        out_shape=out_shape,
        in_specs=[VM] * len(args),
        out_specs=jax.tree.map(lambda _: VM, out_shape),
        compiler_params=pltpu.CompilerParams(vmem_limit_bytes=VMEM_SOME),
        cost_estimate=pl.CostEstimate(flops=10**7, bytes_accessed=2 * 2**20, transcendentals=0),
        name=name,
    )(*args)


def project_kernel(place_ref, att_ref, other_ref, w_ref, wo_ref, *refs, fars):
    out_refs, (wo_scr, sems) = refs[: len(fars)], refs[len(fars) :]
    k = place_ref[1]
    cols = [pl.ds(pl.multiple_of((2 * ((k // 2 + far) % 4) + k % 2) * WIDE, WIDE), WIDE) for far in fars]
    copies = [pltpu.make_async_copy(wo_ref.at[:, c], wo_scr.at[n], sems.at[n]) for n, c in enumerate(cols)]
    for copy in copies:
        copy.start()
    for c, copy, wo, out_ref in zip(cols, copies, range(len(fars)), out_refs):
        value = jnp.dot(att_ref[...], w_ref[:, c], preferred_element_type=F32)
        copy.wait()
        value = value + jnp.dot(other_ref[...], wo_scr[wo], preferred_element_type=F32)
        out_ref[...] = value.astype(out_ref.dtype)


def project(place, att, other, w, wo, fars, dtypes):
    rows, depth = att.shape
    return pl.pallas_call(
        functools.partial(project_kernel, fars=fars),
        out_shape=[jax.ShapeDtypeStruct((rows, WIDE), t) for t in dtypes],
        in_specs=[SM, VM, VM, VM, HB],
        out_specs=[VM] * len(fars),
        scratch_shapes=[
            pltpu.VMEM((len(fars), depth, WIDE), BF),
            pltpu.SemaphoreType.DMA((len(fars),)),
        ],
        compiler_params=pltpu.CompilerParams(vmem_limit_bytes=30 * 2**20),
        cost_estimate=pl.CostEstimate(flops=3 * 10**9 * len(fars), bytes_accessed=2**20, transcendentals=0),
        name="project",
    )(place, att, other, w, wo)


def body(queries, kv_cache, block_list, out_weight):
    s = lax.axis_index("seq")
    k = lax.axis_index("kvh")
    last = lax.axis_size("seq") - 1
    place = jnp.stack([s, k, jnp.where(s == last, 1, 0)]).astype(jnp.int32)
    kv = kv_cache[0]
    w = out_weight[0]
    block_count = kv.shape[0] // BLK
    qb_count = block_list.shape[0]

    def zx(v, dz, dx):
        return lax.ppermute(v, "seq", seq_shift(dz % 4, dx % 4))

    def flip(v, fz, fx):
        return lax.ppermute(v, "seq", seq_flip(fz, fx))

    def yc(v, dy, dc):
        return lax.ppermute(v, "kvh", kvh_shift(dy % 4, dc))

    w_other = yc(w, 0, 1)

    q = queries[:, 0, :].reshape(2, BLK, GROUP * HD)
    a, b = q[0:1], q[1:2]
    a, b = lax.optimization_barrier((jnp.concatenate([a, flip(a, 0, 1)]), jnp.concatenate([b, flip(b, 1, 0)])))
    a, b = lax.optimization_barrier((jnp.concatenate([a, flip(a, 0, 3)]), jnp.concatenate([b, flip(b, 3, 0)])))
    au, bu, ad, bd = lax.optimization_barrier((zx(a, 1, 0), zx(b, 0, 1), zx(a, -1, 0), zx(b, 0, -1)))
    af, bf = zx(au, 1, 0), zx(bu, 0, 1)

    own_ids = (last + 1) * block_count - qb_count + jnp.arange(qb_count, dtype=jnp.int32)
    diag_here = (s == last).astype(jnp.int32)
    mine = (block_list // block_count == s) & (block_list != own_ids[:, None])
    rank = jnp.cumsum(mine.astype(jnp.int32), axis=1) - 1 + diag_here
    counts = jnp.sum(mine.astype(jnp.int32), axis=1) + diag_here
    slots = jnp.arange(MOST, dtype=jnp.int32)
    hit = mine[:, :, None] & (rank[:, :, None] == slots[None, None, :])
    ids = jnp.sum(jnp.where(hit, (block_list % block_count)[:, :, None], 0), axis=1)
    ids = jnp.where((slots[None, :] == 0) & (diag_here == 1), (own_ids % block_count)[:, None], ids)
    ids = ids.reshape(-1)

    def run(pair, far, dtype, cut=1):
        return attend(place, counts, ids, kv, pair, far, dtype, cut)

    ra1, rb1 = run([au, bu], 1, F32)
    ra3, rb3 = run([ad, bd], 3, F32)
    ra2_lo, ra2_hi, rb2_lo, rb2_hi = run([af, bf], 2, BF, 2)
    ra2_lo, ra2_hi = zx(ra2_lo, -1, 0), zx(ra2_hi, 1, 0)
    rb2_lo, rb2_hi = zx(rb2_lo, 0, -1), zx(rb2_hi, 0, 1)
    ao, bo = run([a, b], 0, F32)
    b_four, b_one = (jax.ShapeDtypeStruct((n, PAY, ROWS), BF) for n in (4, 1))
    f_one = jax.ShapeDtypeStruct((1, PAY, ROWS), F32)
    ra1, ra3, rb1, rb3 = local_call(
        join_kernel, [b_four] * 4, [ra1, ra3, ra2_lo, ra2_hi, rb1, rb3, rb2_lo, rb2_hi], "join"
    )
    ra1, rb1, ra3, rb3 = zx(ra1, -1, 0), zx(rb1, 0, -1), zx(ra3, 1, 0), zx(rb3, 0, 1)
    stage_in = [ao, ra3, ra1, bo, rb3, rb1]
    m = local_call(stage_kernel, [f_one, b_one, b_one, b_one] * 2, stage_in, "stage")
    final_in = [m[0]] + [flip(m[n], 0, FLIPS[n]) for n in (1, 2, 3)]
    final_in += [m[4]] + [flip(m[4 + n], FLIPS[n], 0) for n in (1, 2, 3)]
    att = local_call(final_kernel, jax.ShapeDtypeStruct((2 * BLK, GROUP * HD), BF), final_in, "final")

    other = yc(att, 0, 1)

    p1, p3 = project(place, att, other, w, w_other, (1, 3), (BF, BF))
    r1, r3 = yc(p1, 1, 0), yc(p3, 3, 0)
    (p2,) = project(place, att, other, w, w_other, (2,), (BF,))
    r2 = yc(p2, 2, 0)
    (own,) = project(place, att, other, w, w_other, (0,), (F32,))
    return own + r1.astype(F32) + r2.astype(F32) + r3.astype(F32)


def solution(mesh):
    in_specs = (P("seq", "kvh", None), P("kvh", "seq", None), P(), P("kvh", None, None))
    out_specs = P("seq", "kvh")
    return jax.shard_map(body, mesh=mesh, in_specs=in_specs, out_specs=out_specs, check_vma=False)
```

```python
import functools
import math

import jax
import jax.numpy as jnp
from jax import lax
from jax.experimental import pallas as pl
from jax.experimental.pallas import tpu as pltpu
from jax.sharding import PartitionSpec as P

BLK = 64
MOST = 16
HD = 128
GROUP = 8
ROWS = BLK * GROUP
CHUNK = 4
FLIPS = (0, 1, 3, 2)
PAY = HD + 16
NEG = -1e30
SCALE = 1.0 / math.sqrt(HD)
LOG2E = math.log2(math.e)
BF = jnp.bfloat16
F32 = jnp.float32
COST = 4 * 10**9
VMEM_SOME = 16 * 2**20


def seq_shift(dz, dx):
    return [(z * 4 + x, ((z + dz) % 4) * 4 + (x + dx) % 4) for z in range(4) for x in range(4)]


def seq_flip(fz, fx):
    return [(z * 4 + x, (z ^ fz) * 4 + (x ^ fx)) for z in range(4) for x in range(4)]


def kvh_shift(dy, dc):
    return [(y * 2 + c, ((y + dy) % 4) * 2 + (c + dc) % 2) for y in range(4) for c in range(2)]


def pack(numer, peak, total):
    high = total.astype(BF).astype(F32)
    low = total - high
    row = lax.broadcasted_iota(jnp.int32, (16, ROWS), 0)
    tail = jnp.where(row == 0, peak, jnp.where(row == 1, high, jnp.where(row == 2, low, 0.0)))
    return numer, tail


def attend_kernel(place_ref, count_ref, ids_ref, kv_ref, *refs, far, cut):
    parts, per = 2, 4
    q_refs, refs = refs[:parts], refs[parts:]
    out_refs, refs = refs[: parts * cut], refs[parts * cut :]
    q_scr, o_scr, s_scr, diag_scr = refs
    total = parts * per
    pairs = total // 2
    step = CHUNK * BLK

    place = place_ref[0]
    z, x = place // 4, place % 4

    def qb_of(t):
        j = t % per
        f = j ^ (j // 2)
        qa = 2 * (((z + 4 - far) % 4) * 4 + (x ^ f))
        qb = 2 * ((z ^ f) * 4 + (x + 4 - far) % 4) + 1
        return jnp.where(t < per, qa, qb)

    def size(p):
        most = jnp.maximum(count_ref[qb_of(2 * p)], count_ref[qb_of(2 * p + 1)])
        return jnp.where(most <= CHUNK, 1, jnp.where(most <= 2 * CHUNK, 2, MOST // CHUNK))

    off = lax.broadcasted_iota(jnp.int32, (BLK, ROWS), 0)
    tok = lax.broadcasted_iota(jnp.int32, (BLK, ROWS), 1) % BLK
    diag_scr[...] = jnp.where((off > tok) & (place_ref[2] == 1), NEG, 0.0)
    for i, q_ref in enumerate(q_refs):
        q_scr[i * per : (i + 1) * per] = q_ref[...]

    def work(p, chunks):
        qbs = [qb_of(2 * p + u) for u in range(2)]
        counts = [count_ref[qb] for qb in qbs]

        def fetch(u, c, lo):
            ids = [ids_ref[qbs[u] * MOST + c * CHUNK + v] for v in range(CHUNK)]
            return jnp.concatenate(
                [kv_ref[pl.ds(pl.multiple_of(i * BLK, BLK), BLK), lo : lo + HD] for i in ids], axis=0
            )

        peaks = []
        for u in range(2):
            q = jnp.concatenate([q_scr[2 * p + u, :, g * HD : (g + 1) * HD] for g in range(GROUP)], axis=0)
            peak = None
            for c in range(chunks):
                s = lax.dot_general(
                    fetch(u, c, 0),
                    q,
                    (((1,), (1,)), ((), ())),
                    preferred_element_type=F32,
                )
                for v in range(CHUNK):
                    at = c * CHUNK + v
                    part = s[v * BLK : (v + 1) * BLK]
                    if at == 0:
                        part = part + diag_scr[...]
                    else:
                        part = part + jnp.where(at < counts[u], 0.0, NEG)
                    s_scr[u, at * BLK : (at + 1) * BLK, :] = part
                    part = jnp.max(part.reshape(BLK // 8, 8, ROWS), axis=0)
                    peak = part if peak is None else jnp.maximum(peak, part)
            peaks.append(jnp.max(peak, axis=0, keepdims=True))
        for u in range(2):
            peak = peaks[u]
            numer, mass = None, None
            for c in range(chunks):
                w = jnp.exp2((s_scr[u, c * step : (c + 1) * step, :] - peak) * (SCALE * LOG2E))
                part = lax.dot_general(
                    fetch(u, c, HD),
                    w.astype(BF),
                    (((0,), (0,)), ((), ())),
                    preferred_element_type=F32,
                )
                numer = part if numer is None else numer + part
                part = jnp.sum(w.reshape(step // 8, 8, ROWS), axis=0)
                mass = part if mass is None else mass + part
            mass = jnp.sum(mass, axis=0, keepdims=True)
            used = counts[u] > 0
            scaled = peak * SCALE
            near = scaled.astype(BF).astype(F32)
            gain = jnp.where(used, jnp.exp2((scaled - near) * LOG2E), 0.0)
            near = jnp.where(used, near, NEG)
            numer, mass = numer * gain, mass * gain
            numer, tail = pack(numer, near, mass)
            o_scr[2 * p + u, :HD] = numer.astype(o_scr.dtype)
            o_scr[2 * p + u, HD:] = tail.astype(o_scr.dtype)

    def one(p, carry):
        have = size(p)
        for chunks in (1, 2, MOST // CHUNK):

            @pl.when(have == chunks)
            def _(chunks=chunks):
                work(p, chunks)

        return carry

    lax.fori_loop(0, pairs, one, 0)
    for i, out_ref in enumerate(out_refs):
        out_ref[...] = o_scr[i * per // cut : (i + 1) * per // cut]


VM = pl.BlockSpec(memory_space=pltpu.VMEM)
SM = pl.BlockSpec(memory_space=pltpu.SMEM)


HB = pl.BlockSpec(memory_space=pltpu.HBM)
WIDE = 1024


def attend(place, counts, ids, kv, arrays, far, dtype, cut):
    parts, per = 2, 4
    total = parts * per
    return pl.pallas_call(
        functools.partial(attend_kernel, far=far, cut=cut),
        out_shape=[jax.ShapeDtypeStruct((per // cut, PAY, ROWS), dtype)] * (parts * cut),
        in_specs=[SM, SM, SM, VM] + [VM] * parts,
        out_specs=[VM] * (parts * cut),
        scratch_shapes=[
            pltpu.VMEM((total, BLK, GROUP * HD), BF),
            pltpu.VMEM((total, PAY, ROWS), dtype),
            pltpu.VMEM((2, MOST * BLK, ROWS), F32),
            pltpu.VMEM((BLK, ROWS), F32),
        ],
        compiler_params=pltpu.CompilerParams(vmem_limit_bytes=VMEM_SOME),
        cost_estimate=pl.CostEstimate(flops=COST, bytes_accessed=2**20, transcendentals=0),
        name="attend",
    )(place, counts, ids, kv, *arrays)


def merge(blocks):
    tails = [b[HD:].astype(F32) for b in blocks]
    peaks = [t[0:1] for t in tails]
    top = functools.reduce(jnp.maximum, peaks)
    gains = [jnp.exp2((p - top) * LOG2E) for p in peaks]
    numer = sum(b[:HD].astype(F32) * g for b, g in zip(blocks, gains))
    total = sum((t[1:2] + t[2:3]) * g for t, g in zip(tails, gains))
    return numer, top, total


def store(out, at, numer, peak, total):
    numer, tail = pack(numer, peak, total)
    out[at, :HD] = numer.astype(out.dtype)
    out[at, HD:] = tail.astype(out.dtype)


def join_kernel(*refs):
    ins, outs = refs[:8], refs[8:]
    for half in range(2):
        low, high, far_lo, far_hi = ins[half * 4 : half * 4 + 4]
        low_out, high_out = outs[half * 2 : half * 2 + 2]
        for slot in range(4):
            store(low_out, slot, *merge([low[slot], far_lo[slot]] if slot < 2 else [low[slot]]))
            store(high_out, slot, *merge([high[slot], far_hi[slot - 2]] if slot > 1 else [high[slot]]))


def stage_kernel(*refs):
    ins, outs = refs[:6], refs[6:]
    for half in range(2):
        for slot in range(4):
            store(outs[half * 4 + slot], 0, *merge([r[slot] for r in ins[half * 3 : half * 3 + 3]]))


def final_kernel(*refs):
    ins, out = refs[:8], refs[8]
    for half in range(2):
        numer, _, total = merge([r[0] for r in ins[half * 4 : half * 4 + 4]])
        att = numer / total
        for g in range(0, GROUP, 2):
            turned = att[:, g * BLK : (g + 2) * BLK].T.astype(BF)
            out[half * BLK : (half + 1) * BLK, g * HD : (g + 1) * HD] = turned[:BLK]
            out[half * BLK : (half + 1) * BLK, (g + 1) * HD : (g + 2) * HD] = turned[BLK:]


def local_call(kernel, out_shape, args, name):
    return pl.pallas_call(
        kernel,
        out_shape=out_shape,
        in_specs=[VM] * len(args),
        out_specs=jax.tree.map(lambda _: VM, out_shape),
        compiler_params=pltpu.CompilerParams(vmem_limit_bytes=VMEM_SOME),
        cost_estimate=pl.CostEstimate(flops=10**7, bytes_accessed=2 * 2**20, transcendentals=0),
        name=name,
    )(*args)


def project_kernel(place_ref, att_ref, other_ref, w_ref, wo_ref, *refs, fars):
    out_refs, (wo_scr, sems) = refs[: len(fars)], refs[len(fars) :]
    k = place_ref[1]
    cols = [pl.ds(pl.multiple_of((2 * ((k // 2 + far) % 4) + k % 2) * WIDE, WIDE), WIDE) for far in fars]
    copies = [pltpu.make_async_copy(wo_ref.at[:, c], wo_scr.at[n], sems.at[n]) for n, c in enumerate(cols)]
    for copy in copies:
        copy.start()
    for c, copy, wo, out_ref in zip(cols, copies, range(len(fars)), out_refs):
        value = jnp.dot(att_ref[...], w_ref[:, c], preferred_element_type=F32)
        copy.wait()
        value = value + jnp.dot(other_ref[...], wo_scr[wo], preferred_element_type=F32)
        out_ref[...] = value.astype(out_ref.dtype)


def project(place, att, other, w, wo, fars, dtypes):
    rows, depth = att.shape
    return pl.pallas_call(
        functools.partial(project_kernel, fars=fars),
        out_shape=[jax.ShapeDtypeStruct((rows, WIDE), t) for t in dtypes],
        in_specs=[SM, VM, VM, VM, HB],
        out_specs=[VM] * len(fars),
        scratch_shapes=[
            pltpu.VMEM((len(fars), depth, WIDE), BF),
            pltpu.SemaphoreType.DMA((len(fars),)),
        ],
        compiler_params=pltpu.CompilerParams(vmem_limit_bytes=30 * 2**20),
        cost_estimate=pl.CostEstimate(flops=3 * 10**9 * len(fars), bytes_accessed=2**20, transcendentals=0),
        name="project",
    )(place, att, other, w, wo)


def body(queries, kv_cache, block_list, out_weight):
    s = lax.axis_index("seq")
    k = lax.axis_index("kvh")
    last = lax.axis_size("seq") - 1
    place = jnp.stack([s, k, jnp.where(s == last, 1, 0)]).astype(jnp.int32)
    kv = kv_cache[0]
    w = out_weight[0]
    block_count = kv.shape[0] // BLK
    qb_count = block_list.shape[0]

    def zx(v, dz, dx):
        return lax.ppermute(v, "seq", seq_shift(dz % 4, dx % 4))

    def flip(v, fz, fx):
        return lax.ppermute(v, "seq", seq_flip(fz, fx))

    def yc(v, dy, dc):
        return lax.ppermute(v, "kvh", kvh_shift(dy % 4, dc))

    w_other = yc(w, 0, 1)

    q = queries[:, 0, :].reshape(2, BLK, GROUP * HD)
    a, b = q[0:1], q[1:2]
    a, b = lax.optimization_barrier((jnp.concatenate([a, flip(a, 0, 1)]), jnp.concatenate([b, flip(b, 1, 0)])))
    a, b = lax.optimization_barrier((jnp.concatenate([a, flip(a, 0, 3)]), jnp.concatenate([b, flip(b, 3, 0)])))
    au, bu, ad, bd = zx(a, 1, 0), zx(b, 0, 1), zx(a, -1, 0), zx(b, 0, -1)
    af, bf = zx(au, 1, 0), zx(bu, 0, 1)

    own_ids = (last + 1) * block_count - qb_count + jnp.arange(qb_count, dtype=jnp.int32)
    diag_here = (s == last).astype(jnp.int32)
    mine = (block_list // block_count == s) & (block_list != own_ids[:, None])
    rank = jnp.cumsum(mine.astype(jnp.int32), axis=1) - 1 + diag_here
    counts = jnp.sum(mine.astype(jnp.int32), axis=1) + diag_here
    slots = jnp.arange(MOST, dtype=jnp.int32)
    hit = mine[:, :, None] & (rank[:, :, None] == slots[None, None, :])
    ids = jnp.sum(jnp.where(hit, (block_list % block_count)[:, :, None], 0), axis=1)
    ids = jnp.where((slots[None, :] == 0) & (diag_here == 1), (own_ids % block_count)[:, None], ids)
    ids = ids.reshape(-1)

    def run(pair, far, dtype, cut=1):
        return attend(place, counts, ids, kv, pair, far, dtype, cut)

    ra1, rb1 = run([au, bu], 1, F32)
    ra3, rb3 = run([ad, bd], 3, F32)
    ra2_lo, ra2_hi, rb2_lo, rb2_hi = run([af, bf], 2, BF, 2)
    ra2_lo, ra2_hi = zx(ra2_lo, -1, 0), zx(ra2_hi, 1, 0)
    rb2_lo, rb2_hi = zx(rb2_lo, 0, -1), zx(rb2_hi, 0, 1)
    ao, bo = run([a, b], 0, F32)
    b_four, b_one = (jax.ShapeDtypeStruct((n, PAY, ROWS), BF) for n in (4, 1))
    f_one = jax.ShapeDtypeStruct((1, PAY, ROWS), F32)
    ra1, ra3, rb1, rb3 = local_call(
        join_kernel, [b_four] * 4, [ra1, ra3, ra2_lo, ra2_hi, rb1, rb3, rb2_lo, rb2_hi], "join"
    )
    ra1, rb1, ra3, rb3 = zx(ra1, -1, 0), zx(rb1, 0, -1), zx(ra3, 1, 0), zx(rb3, 0, 1)
    stage_in = [ao, ra3, ra1, bo, rb3, rb1]
    m = local_call(stage_kernel, [f_one, b_one, b_one, b_one] * 2, stage_in, "stage")
    final_in = [m[0]] + [flip(m[n], 0, FLIPS[n]) for n in (1, 2, 3)]
    final_in += [m[4]] + [flip(m[4 + n], FLIPS[n], 0) for n in (1, 2, 3)]
    att = local_call(final_kernel, jax.ShapeDtypeStruct((2 * BLK, GROUP * HD), BF), final_in, "final")

    other = yc(att, 0, 1)

    p1, p3 = project(place, att, other, w, w_other, (1, 3), (BF, BF))
    r1, r3 = yc(p1, 1, 0), yc(p3, 3, 0)
    (p2,) = project(place, att, other, w, w_other, (2,), (BF,))
    r2 = yc(p2, 2, 0)
    (own,) = project(place, att, other, w, w_other, (0,), (F32,))
    return own + r1.astype(F32) + r2.astype(F32) + r3.astype(F32)


def solution(mesh):
    in_specs = (P("seq", "kvh", None), P("kvh", "seq", None), P(), P("kvh", None, None))
    out_specs = P("seq", "kvh")
    return jax.shard_map(body, mesh=mesh, in_specs=in_specs, out_specs=out_specs, check_vma=False)
```

```python
import functools
import math

import jax
import jax.numpy as jnp
from jax import lax
from jax.experimental import pallas as pl
from jax.experimental.pallas import tpu as pltpu
from jax.sharding import PartitionSpec as P

BLK = 64
MOST = 16
HD = 128
GROUP = 8
ROWS = BLK * GROUP
CHUNK = 4
FLIPS = (0, 1, 3, 2)
PAY = HD + 16
NEG = -1e30
SCALE = 1.0 / math.sqrt(HD)
LOG2E = math.log2(math.e)
BF = jnp.bfloat16
F32 = jnp.float32
COST = 4 * 10**9
VMEM_SOME = 16 * 2**20


def seq_shift(dz, dx):
    return [(z * 4 + x, ((z + dz) % 4) * 4 + (x + dx) % 4) for z in range(4) for x in range(4)]


def seq_flip(fz, fx):
    return [(z * 4 + x, (z ^ fz) * 4 + (x ^ fx)) for z in range(4) for x in range(4)]


def kvh_shift(dy, dc):
    return [(y * 2 + c, ((y + dy) % 4) * 2 + (c + dc) % 2) for y in range(4) for c in range(2)]


def pack(numer, peak, total):
    high = total.astype(BF).astype(F32)
    low = total - high
    row = lax.broadcasted_iota(jnp.int32, (16, ROWS), 0)
    tail = jnp.where(row == 0, peak, jnp.where(row == 1, high, jnp.where(row == 2, low, 0.0)))
    return numer, tail


def attend_kernel(place_ref, count_ref, ids_ref, kv_ref, *refs, far, cut):
    parts, per = 2, 4
    q_refs, refs = refs[:parts], refs[parts:]
    out_refs, refs = refs[: parts * cut], refs[parts * cut :]
    q_scr, o_scr, s_scr, diag_scr = refs
    total = parts * per
    pairs = total // 2
    step = CHUNK * BLK

    place = place_ref[0]
    z, x = place // 4, place % 4

    def qb_of(t):
        j = t % per
        f = j ^ (j // 2)
        qa = 2 * (((z + 4 - far) % 4) * 4 + (x ^ f))
        qb = 2 * ((z ^ f) * 4 + (x + 4 - far) % 4) + 1
        return jnp.where(t < per, qa, qb)

    def size(p):
        most = jnp.maximum(count_ref[qb_of(2 * p)], count_ref[qb_of(2 * p + 1)])
        return jnp.where(most <= CHUNK, 1, jnp.where(most <= 2 * CHUNK, 2, MOST // CHUNK))

    off = lax.broadcasted_iota(jnp.int32, (BLK, ROWS), 0)
    tok = lax.broadcasted_iota(jnp.int32, (BLK, ROWS), 1) % BLK
    diag_scr[...] = jnp.where((off > tok) & (place_ref[2] == 1), NEG, 0.0)
    for i, q_ref in enumerate(q_refs):
        q_scr[i * per : (i + 1) * per] = q_ref[...]

    def work(p, chunks):
        qbs = [qb_of(2 * p + u) for u in range(2)]
        counts = [count_ref[qb] for qb in qbs]

        def fetch(u, c, lo):
            ids = [ids_ref[qbs[u] * MOST + c * CHUNK + v] for v in range(CHUNK)]
            return jnp.concatenate(
                [kv_ref[pl.ds(pl.multiple_of(i * BLK, BLK), BLK), lo : lo + HD] for i in ids], axis=0
            )

        peaks = []
        for u in range(2):
            q = jnp.concatenate([q_scr[2 * p + u, :, g * HD : (g + 1) * HD] for g in range(GROUP)], axis=0)
            peak = None
            for c in range(chunks):
                s = lax.dot_general(
                    fetch(u, c, 0),
                    q,
                    (((1,), (1,)), ((), ())),
                    preferred_element_type=F32,
                )
                for v in range(CHUNK):
                    at = c * CHUNK + v
                    part = s[v * BLK : (v + 1) * BLK]
                    if at == 0:
                        part = part + diag_scr[...]
                    else:
                        part = part + jnp.where(at < counts[u], 0.0, NEG)
                    s_scr[u, at * BLK : (at + 1) * BLK, :] = part
                    part = jnp.max(part.reshape(BLK // 8, 8, ROWS), axis=0)
                    peak = part if peak is None else jnp.maximum(peak, part)
            peaks.append(jnp.max(peak, axis=0, keepdims=True))
        for u in range(2):
            peak = peaks[u]
            numer, mass = None, None
            for c in range(chunks):
                w = jnp.exp2((s_scr[u, c * step : (c + 1) * step, :] - peak) * (SCALE * LOG2E))
                part = lax.dot_general(
                    fetch(u, c, HD),
                    w.astype(BF),
                    (((0,), (0,)), ((), ())),
                    preferred_element_type=F32,
                )
                numer = part if numer is None else numer + part
                part = jnp.sum(w.reshape(step // 8, 8, ROWS), axis=0)
                mass = part if mass is None else mass + part
            mass = jnp.sum(mass, axis=0, keepdims=True)
            used = counts[u] > 0
            scaled = peak * SCALE
            near = scaled.astype(BF).astype(F32)
            gain = jnp.where(used, jnp.exp2((scaled - near) * LOG2E), 0.0)
            near = jnp.where(used, near, NEG)
            numer, mass = numer * gain, mass * gain
            numer, tail = pack(numer, near, mass)
            o_scr[2 * p + u, :HD] = numer.astype(o_scr.dtype)
            o_scr[2 * p + u, HD:] = tail.astype(o_scr.dtype)

    def one(p, carry):
        have = size(p)
        for chunks in (1, 2, MOST // CHUNK):

            @pl.when(have == chunks)
            def _(chunks=chunks):
                work(p, chunks)

        return carry

    lax.fori_loop(0, pairs, one, 0)
    for i, out_ref in enumerate(out_refs):
        out_ref[...] = o_scr[i * per // cut : (i + 1) * per // cut]


VM = pl.BlockSpec(memory_space=pltpu.VMEM)
SM = pl.BlockSpec(memory_space=pltpu.SMEM)


HB = pl.BlockSpec(memory_space=pltpu.HBM)
WIDE = 1024


def attend(place, counts, ids, kv, arrays, far, dtype, cut):
    parts, per = 2, 4
    total = parts * per
    return pl.pallas_call(
        functools.partial(attend_kernel, far=far, cut=cut),
        out_shape=[jax.ShapeDtypeStruct((per // cut, PAY, ROWS), dtype)] * (parts * cut),
        in_specs=[SM, SM, SM, VM] + [VM] * parts,
        out_specs=[VM] * (parts * cut),
        scratch_shapes=[
            pltpu.VMEM((total, BLK, GROUP * HD), BF),
            pltpu.VMEM((total, PAY, ROWS), dtype),
            pltpu.VMEM((2, MOST * BLK, ROWS), F32),
            pltpu.VMEM((BLK, ROWS), F32),
        ],
        compiler_params=pltpu.CompilerParams(vmem_limit_bytes=VMEM_SOME),
        cost_estimate=pl.CostEstimate(flops=COST, bytes_accessed=2**20, transcendentals=0),
        name="attend",
    )(place, counts, ids, kv, *arrays)


def merge(blocks):
    tails = [b[HD:].astype(F32) for b in blocks]
    peaks = [t[0:1] for t in tails]
    top = functools.reduce(jnp.maximum, peaks)
    gains = [jnp.exp2((p - top) * LOG2E) for p in peaks]
    numer = sum(b[:HD].astype(F32) * g for b, g in zip(blocks, gains))
    total = sum((t[1:2] + t[2:3]) * g for t, g in zip(tails, gains))
    return numer, top, total


def store(out, at, numer, peak, total):
    numer, tail = pack(numer, peak, total)
    out[at, :HD] = numer.astype(out.dtype)
    out[at, HD:] = tail.astype(out.dtype)


def join_kernel(*refs):
    ins, outs = refs[:8], refs[8:]
    for half in range(2):
        low, high, far_lo, far_hi = ins[half * 4 : half * 4 + 4]
        low_out, high_out = outs[half * 2 : half * 2 + 2]
        for slot in range(4):
            store(low_out, slot, *merge([low[slot], far_lo[slot]] if slot < 2 else [low[slot]]))
            store(high_out, slot, *merge([high[slot], far_hi[slot - 2]] if slot > 1 else [high[slot]]))


def stage_kernel(*refs):
    ins, outs = refs[:6], refs[6:]
    for half in range(2):
        for slot in range(4):
            store(outs[half * 4 + slot], 0, *merge([r[slot] for r in ins[half * 3 : half * 3 + 3]]))


def final_kernel(*refs):
    ins, out = refs[:8], refs[8]
    for half in range(2):
        numer, _, total = merge([r[0] for r in ins[half * 4 : half * 4 + 4]])
        att = numer / total
        for g in range(0, GROUP, 2):
            turned = att[:, g * BLK : (g + 2) * BLK].T.astype(BF)
            out[half * BLK : (half + 1) * BLK, g * HD : (g + 1) * HD] = turned[:BLK]
            out[half * BLK : (half + 1) * BLK, (g + 1) * HD : (g + 2) * HD] = turned[BLK:]


def local_call(kernel, out_shape, args, name):
    return pl.pallas_call(
        kernel,
        out_shape=out_shape,
        in_specs=[VM] * len(args),
        out_specs=jax.tree.map(lambda _: VM, out_shape),
        compiler_params=pltpu.CompilerParams(vmem_limit_bytes=VMEM_SOME),
        cost_estimate=pl.CostEstimate(flops=10**7, bytes_accessed=2 * 2**20, transcendentals=0),
        name=name,
    )(*args)


PIECES = 2


def project_kernel(place_ref, att_ref, other_ref, w_ref, wo_ref, *refs, fars):
    out_refs, (wo_scr, sems) = refs[: len(fars)], refs[len(fars) :]
    k = place_ref[1]
    cols = [pl.ds(pl.multiple_of((2 * ((k // 2 + far) % 4) + k % 2) * WIDE, WIDE), WIDE) for far in fars]
    rows = wo_ref.shape[0] // PIECES
    copies = [
        [
            pltpu.make_async_copy(
                wo_ref.at[r * rows : (r + 1) * rows, c],
                wo_scr.at[n, r * rows : (r + 1) * rows],
                sems.at[n, r],
            )
            for r in range(PIECES)
        ]
        for n, c in enumerate(cols)
    ]
    for copy in sum(copies, []):
        copy.start()
    for c, copy, wo, out_ref in zip(cols, copies, range(len(fars)), out_refs):
        value = jnp.dot(att_ref[...], w_ref[:, c], preferred_element_type=F32)
        for r in range(PIECES):
            copy[r].wait()
            value = value + jnp.dot(
                other_ref[:, r * rows : (r + 1) * rows],
                wo_scr[wo, r * rows : (r + 1) * rows],
                preferred_element_type=F32,
            )
        out_ref[...] = value.astype(out_ref.dtype)


def project(place, att, other, w, wo, fars, dtypes):
    rows, depth = att.shape
    return pl.pallas_call(
        functools.partial(project_kernel, fars=fars),
        out_shape=[jax.ShapeDtypeStruct((rows, WIDE), t) for t in dtypes],
        in_specs=[SM, VM, VM, VM, HB],
        out_specs=[VM] * len(fars),
        scratch_shapes=[
            pltpu.VMEM((len(fars), depth, WIDE), BF),
            pltpu.SemaphoreType.DMA((len(fars), PIECES)),
        ],
        compiler_params=pltpu.CompilerParams(vmem_limit_bytes=30 * 2**20),
        cost_estimate=pl.CostEstimate(flops=3 * 10**9 * len(fars), bytes_accessed=2**20, transcendentals=0),
        name="project",
    )(place, att, other, w, wo)


def body(queries, kv_cache, block_list, out_weight):
    s = lax.axis_index("seq")
    k = lax.axis_index("kvh")
    last = lax.axis_size("seq") - 1
    place = jnp.stack([s, k, jnp.where(s == last, 1, 0)]).astype(jnp.int32)
    kv = kv_cache[0]
    w = out_weight[0]
    block_count = kv.shape[0] // BLK
    qb_count = block_list.shape[0]

    def zx(v, dz, dx):
        return lax.ppermute(v, "seq", seq_shift(dz % 4, dx % 4))

    def flip(v, fz, fx):
        return lax.ppermute(v, "seq", seq_flip(fz, fx))

    def yc(v, dy, dc):
        return lax.ppermute(v, "kvh", kvh_shift(dy % 4, dc))

    w_other = yc(w, 0, 1)

    q = queries[:, 0, :].reshape(2, BLK, GROUP * HD)
    a, b = q[0:1], q[1:2]
    a, b = lax.optimization_barrier((jnp.concatenate([a, flip(a, 0, 1)]), jnp.concatenate([b, flip(b, 1, 0)])))
    a, b = lax.optimization_barrier((jnp.concatenate([a, flip(a, 0, 3)]), jnp.concatenate([b, flip(b, 3, 0)])))
    au, bu, ad, bd = zx(a, 1, 0), zx(b, 0, 1), zx(a, -1, 0), zx(b, 0, -1)
    af, bf = zx(au, 1, 0), zx(bu, 0, 1)

    own_ids = (last + 1) * block_count - qb_count + jnp.arange(qb_count, dtype=jnp.int32)
    diag_here = (s == last).astype(jnp.int32)
    mine = (block_list // block_count == s) & (block_list != own_ids[:, None])
    rank = jnp.cumsum(mine.astype(jnp.int32), axis=1) - 1 + diag_here
    counts = jnp.sum(mine.astype(jnp.int32), axis=1) + diag_here
    slots = jnp.arange(MOST, dtype=jnp.int32)
    hit = mine[:, :, None] & (rank[:, :, None] == slots[None, None, :])
    ids = jnp.sum(jnp.where(hit, (block_list % block_count)[:, :, None], 0), axis=1)
    ids = jnp.where((slots[None, :] == 0) & (diag_here == 1), (own_ids % block_count)[:, None], ids)
    ids = ids.reshape(-1)

    def run(pair, far, dtype, cut=1):
        return attend(place, counts, ids, kv, pair, far, dtype, cut)

    ra1, rb1 = run([au, bu], 1, F32)
    ra3, rb3 = run([ad, bd], 3, F32)
    ra2_lo, ra2_hi, rb2_lo, rb2_hi = run([af, bf], 2, BF, 2)
    ra2_lo, ra2_hi = zx(ra2_lo, -1, 0), zx(ra2_hi, 1, 0)
    rb2_lo, rb2_hi = zx(rb2_lo, 0, -1), zx(rb2_hi, 0, 1)
    ao, bo = run([a, b], 0, F32)
    b_four, b_one = (jax.ShapeDtypeStruct((n, PAY, ROWS), BF) for n in (4, 1))
    f_one = jax.ShapeDtypeStruct((1, PAY, ROWS), F32)
    ra1, ra3, rb1, rb3 = local_call(
        join_kernel, [b_four] * 4, [ra1, ra3, ra2_lo, ra2_hi, rb1, rb3, rb2_lo, rb2_hi], "join"
    )
    ra1, rb1, ra3, rb3 = zx(ra1, -1, 0), zx(rb1, 0, -1), zx(ra3, 1, 0), zx(rb3, 0, 1)
    stage_in = [ao, ra3, ra1, bo, rb3, rb1]
    m = local_call(stage_kernel, [f_one, b_one, b_one, b_one] * 2, stage_in, "stage")
    final_in = [m[0]] + [flip(m[n], 0, FLIPS[n]) for n in (1, 2, 3)]
    final_in += [m[4]] + [flip(m[4 + n], FLIPS[n], 0) for n in (1, 2, 3)]
    att = local_call(final_kernel, jax.ShapeDtypeStruct((2 * BLK, GROUP * HD), BF), final_in, "final")

    other = yc(att, 0, 1)

    p1, p3 = project(place, att, other, w, w_other, (1, 3), (BF, BF))
    r1, r3 = yc(p1, 1, 0), yc(p3, 3, 0)
    (p2,) = project(place, att, other, w, w_other, (2,), (BF,))
    r2 = yc(p2, 2, 0)
    (own,) = project(place, att, other, w, w_other, (0,), (F32,))
    return own + r1.astype(F32) + r2.astype(F32) + r3.astype(F32)


def solution(mesh):
    in_specs = (P("seq", "kvh", None), P("kvh", "seq", None), P(), P("kvh", None, None))
    out_specs = P("seq", "kvh")
    return jax.shard_map(body, mesh=mesh, in_specs=in_specs, out_specs=out_specs, check_vma=False)
```
